32 devices in a mesh: blk: 8 (over z, x), feat: 4 (over y, core).
Axes of the slice: x: 2, y: 2, z: 4, core: 2. Of those that a mesh axis runs over, the one named last changes fastest.
Arguments:
- features: bfloat16 [8192, 512], P(('blk', 'feat')), may hold values from -8 to 8
- weight: bfloat16 [512, 512], replicated, may hold values from -0.25 to 0.25
- tile_vals: bfloat16 [8, 160, 128, 128], P('blk'), may hold values from 0 to 3, as said below
- pair_counts: int32 [8, 8], P('blk'), may hold values from 0 to 20, as said below
- slot_row: int32 [8, 160], P('blk'), may hold values from 0 to 7
- slot_col: int32 [8, 160], P('blk'), may hold values from 0 to 7
- cotangent: bfloat16 [8192, 512], P('blk', 'feat'), may hold values from -6 to 6
Outputs:
- output: bfloat16 [8192, 512], P('blk', 'feat')
- grad_features: bfloat16 [8192, 512], P(('blk', 'feat'))
- grad_weight: float32 [512, 512], P(None, 'feat')
The draws below stay inside these ranges and needn't reach their ends.
Inputs may be any that keep to these rules, and one draw needn't show every extreme that they name: `pair_counts`: each row block's counts lie between half of a limit drawn for that row block and the limit; every pair (b, b) holds 20 filled slots. `tile_vals`: entries are zero or positive edge weights.
All inputs are finite; a program needn't handle non-finite values.
Results may differ from the reference program's by a relative error of at most 0.018.
Values may be sent and summed in bfloat16 or wider, within the bound.
A program may use at most 128 MiB of HBM per device.

```python
import math
import jax
import jax.numpy as jnp
from jax import lax

D = 512
TILE = 128
ROWS_DEV = 1024
CAP = 20
BLOCKS = 8
TILES_ROW = 8
NODES = 8192


def draw_pair_counts(key, part):
    key_limit, key_count = jax.random.split(key)
    ceiling = jax.random.randint(key_limit, (BLOCKS, 1), (CAP + 3) // 4, CAP + 1)
    counts = jax.random.randint(key_count, (BLOCKS, BLOCKS), ceiling // 2, ceiling + 1)
    diagonal = jnp.arange(BLOCKS)[:, None] == jnp.arange(BLOCKS)[None, :]
    return jnp.where(diagonal, CAP, counts).astype(jnp.int32)


def draw_tile_vals(key, part):
    key_mask, key_value = jax.random.split(key)
    extent = (BLOCKS, BLOCKS * CAP, TILE, TILE)
    spread = max(1, BLOCKS * CAP * TILE // (32 * TILES_ROW))
    present = jax.random.randint(key_mask, extent, 0, spread) == 0
    strength = jnp.exp(jax.random.uniform(key_value, extent, jnp.float32, math.log(0.5), math.log(2.0)))
    return jnp.where(present, strength, 0.0).astype(jnp.bfloat16)


def plant(values, rng, least, top_value):
    shape = values.shape
    index_at = [jax.random.randint(jax.random.fold_in(rng, axis), (), 0, shape[axis]) for axis in range(len(shape))]
    values = values.at[tuple(index_at)].set(least)
    longest = shape.index(max(shape))
    index_at[longest] = (index_at[longest] + 1) % shape[longest]
    return values.at[tuple(index_at)].set(top_value)


def steps_of(stream_key, shape, shards, smallest, high):
    def one(dim, shards_of):
        heights = jax.random.uniform(jax.random.fold_in(jax.random.fold_in(stream_key, 6), dim), (shards_of,), jnp.float32, smallest / len(shards), high / len(shards))
        return jnp.repeat(jnp.exp(heights), shape[dim] // shards_of).reshape((-1,) + (1,) * (len(shape) - dim - 1))

    level = one(*shards[0])
    for cut in shards[1:]:
        level = level * one(*cut)
    return level


def gaussian(rng, dims, scale, reach, cuts=(), held_as=jnp.bfloat16):
    array = jax.random.normal(rng, dims, jnp.float32) * scale
    if len(cuts) > 0:
        array = steps_of(rng, dims, cuts, -0.22, 0.18) * array
    return jnp.clip(array, min=-reach, max=reach).astype(held_as)


def setup_inputs(seed: int = 0) -> dict:
    keys = jax.random.split(jax.random.key(seed), 8)
    return {
        "features": gaussian(keys[0], (NODES, D), 2.0, 8.0, ((0, 32),)),
        "weight": gaussian(keys[1], (D, D), D ** -0.5, 0.25),
        "tile_vals": draw_tile_vals(jax.random.fold_in(keys[7], 71), 0),
        "pair_counts": draw_pair_counts(jax.random.fold_in(keys[7], 71), 0),
        "slot_row": plant(jax.random.randint(keys[4], (BLOCKS, BLOCKS * CAP), 0, TILES_ROW), jax.random.fold_in(keys[4], 1), 0, TILES_ROW - 1).astype(jnp.int32),
        "slot_col": plant(jax.random.randint(keys[5], (BLOCKS, BLOCKS * CAP), 0, TILES_ROW), jax.random.fold_in(keys[5], 1), 0, TILES_ROW - 1).astype(jnp.int32),
        "cotangent": gaussian(keys[6], (NODES, D), 1.0, 6.0, ((0, 8), (1, 4))),
    }


def activation(values):
    return jax.nn.gelu(values, approximate=True)

def node_degrees(tile_vals, pair_counts, slot_row):

    def per_block(inputs):
        values, counts, row_ids = inputs
        filled = (jnp.arange(BLOCKS * CAP, dtype=jnp.int32) % CAP < jnp.repeat(counts, CAP)).astype(jnp.float32)
        row_sums = lax.optimization_barrier(jnp.sum(values.astype(jnp.float32), axis=2)) * filled[:, None]
        degree = jnp.zeros((TILES_ROW, TILE), jnp.float32).at[row_ids].add(row_sums)
        return (1.0 + degree).reshape(ROWS_DEV)
    return lax.map(per_block, (tile_vals, pair_counts, slot_row)).reshape(NODES)

def adjacency_times(tile_vals, pair_counts, slot_row, slot_col, scaled):
    tiled = scaled.astype(jnp.float32).reshape(BLOCKS * TILES_ROW, TILE, D)

    def per_block(inputs):
        values, counts, row_ids, col_ids = inputs

        def advance(running, column):
            first = (column * CAP).astype(jnp.int32)
            chosen = lax.dynamic_slice_in_dim(values, first, CAP, 0).astype(jnp.float32)
            rows_here = lax.dynamic_slice_in_dim(row_ids, first, CAP, 0)
            cols_here = lax.dynamic_slice_in_dim(col_ids, first, CAP, 0)
            filled = (jnp.arange(CAP, dtype=jnp.int32) < counts[column]).astype(jnp.float32)
            picked = tiled[(column * TILES_ROW + cols_here).astype(jnp.int32)]
            product = jnp.einsum('sij,sjf->sif', chosen, picked, precision=lax.Precision.HIGHEST)
            return (running.at[rows_here].add(product * filled[:, None, None]), None)
        running, _ = lax.scan(advance, jnp.zeros((TILES_ROW, TILE, D), jnp.float32), jnp.arange(BLOCKS, dtype=jnp.int32))
        return running.reshape(ROWS_DEV, D)
    return lax.map(per_block, (tile_vals, pair_counts, slot_row, slot_col)).reshape(NODES, D)

def adjacency_transposed(tile_vals, pair_counts, slot_row, slot_col, grads):
    tiled = grads.astype(jnp.float32).reshape(BLOCKS * TILES_ROW, TILE, D)
    zero = jnp.zeros((), jnp.int32)

    def per_column(column):

        def advance(running, block_id):
            first = (column * CAP).astype(jnp.int32)
            block_index = block_id.astype(jnp.int32)
            column_index = column.astype(jnp.int32)
            chosen = lax.dynamic_slice(tile_vals, (block_index, first, zero, zero), (1, CAP, TILE, TILE))[0].astype(jnp.float32)
            rows_here = lax.dynamic_slice(slot_row, (block_index, first), (1, CAP))[0]
            cols_here = lax.dynamic_slice(slot_col, (block_index, first), (1, CAP))[0]
            count_here = lax.dynamic_slice(pair_counts, (block_index, column_index), (1, 1))[0, 0]
            filled = (jnp.arange(CAP, dtype=jnp.int32) < count_here).astype(jnp.float32)
            picked = tiled[(block_index * TILES_ROW + rows_here).astype(jnp.int32)]
            product = jnp.einsum('sij,sif->sjf', chosen, picked, precision=lax.Precision.HIGHEST)
            block_term = jnp.zeros((TILES_ROW, TILE, D), jnp.float32).at[cols_here].add(product * filled[:, None, None])
            rounded = lax.optimization_barrier(block_term.astype(jnp.bfloat16)).astype(jnp.float32)
            return (running + rounded, None)
        running, _ = lax.scan(advance, jnp.zeros((TILES_ROW, TILE, D), jnp.float32), jnp.arange(BLOCKS, dtype=jnp.int32))
        return running.reshape(ROWS_DEV, D)
    return lax.map(per_column, jnp.arange(BLOCKS, dtype=jnp.int32)).reshape(NODES, D)

def reference(features, weight, tile_vals, pair_counts, slot_row, slot_col, cotangent):
    degree = node_degrees(tile_vals, pair_counts, slot_row)
    scaling = lax.rsqrt(degree)
    hidden = jnp.dot(features, weight, preferred_element_type=jnp.float32)
    scaled = (scaling[:, None] * hidden).astype(jnp.bfloat16)
    summed = adjacency_times(tile_vals, pair_counts, slot_row, slot_col, scaled)
    preact = scaling[:, None] * (summed + scaled.astype(jnp.float32))
    output = activation(preact).astype(jnp.bfloat16)
    grad_preact = jax.vjp(activation, preact)[1](cotangent.astype(jnp.float32))[0]
    scaled_grad = (scaling[:, None] * grad_preact).astype(jnp.bfloat16)
    back_sums = adjacency_transposed(tile_vals, pair_counts, slot_row, slot_col, scaled_grad)
    hidden_grad = (scaling[:, None] * (back_sums + scaled_grad.astype(jnp.float32))).astype(jnp.bfloat16)
    grad_features = jnp.dot(hidden_grad, weight.T, preferred_element_type=jnp.float32).astype(jnp.bfloat16)
    grad_weight = jnp.dot(features.T, hidden_grad, preferred_element_type=jnp.float32) * NODES ** (-0.5)
    return (output, grad_features, grad_weight)
```

```python
import functools

import jax
import jax.numpy as jnp
from jax import lax
from jax.experimental import pallas as pl
from jax.experimental.pallas import tpu as pltpu
from jax.sharding import PartitionSpec as P

MESH = pl.DeviceIdType.MESH
VMEM = pl.BlockSpec(memory_space=pltpu.VMEM)
F32, BF16 = jnp.float32, jnp.bfloat16
LIMIT = 56 * 1024 * 1024
CUTS = 2
GELU_C = 0.7978845608028654
GELU_A = 0.044715


def ring_of(n):
    me = lax.axis_index("blk")
    half = n // 2
    pos = jnp.where(me % 2 == 0, me // 2, n - 1 - me // 2)

    def blk_of(p):
        p = (p + 2 * n) % n
        return jnp.where(p < half, 2 * p, 2 * (n - 1 - p) + 1)

    return me, pos, blk_of


def greet(peers):
    barrier = pltpu.get_barrier_semaphore()
    for peer in peers:
        pl.semaphore_signal(barrier, inc=1, device_id=peer, device_id_type=MESH)
    pl.semaphore_wait(barrier, len(peers))


def remote(src, dst, send, recv, peer):
    return pltpu.make_async_remote_copy(
        src_ref=src, dst_ref=dst, send_sem=send, recv_sem=recv, device_id=peer, device_id_type=MESH
    )


def scaling_kernel(steps, per, tiles_row, rows_ref, tiles_ref, sc_ref, sct_ref, acc):
    step = pl.program_id(0)

    @pl.when(step == 0)
    def _():
        acc[...] = jnp.zeros_like(acc)

    for k in range(per):
        acc[rows_ref[step * per + k]] += tiles_ref[k].astype(F32)

    @pl.when(step == steps - 1)
    def _():
        for t in range(tiles_row):
            degree = 1.0 + jnp.sum(acc[t], axis=1, keepdims=True)
            wide = jnp.broadcast_to(lax.rsqrt(degree), acc.shape[1:])
            sc_ref[t] = wide
            sct_ref[t] = wide.T[0:8]


def gather_kernel(n, nf, feat_ref, w_ref, sc_ref, all_ref, fb_ref, buf, as_, ar, fs, fr, rs, rr):
    me, pos, blk_of = ring_of(n)
    mf = lax.axis_index("feat")
    quarter = feat_ref.shape[0]
    cols = all_ref.shape[2]
    right, left = (blk_of(pos + 1), mf), (blk_of(pos - 1), mf)
    peers = [(me, (mf + d) % nf) for d in range(1, nf)]
    greet(peers + [right, left])
    mine = pl.ds(pl.multiple_of(mf * quarter, quarter), quarter)
    scale = sc_ref[mine, :]

    def rows_for(f):
        w = w_ref[:, pl.ds(pl.multiple_of(f * cols, cols), cols)]
        h = jnp.dot(feat_ref[...], w, preferred_element_type=F32)
        return (scale * h).astype(BF16)

    first = []
    for d in (2, 3, 1):
        peer = peers[d - 1]
        buf[d - 1] = rows_for(peer[1])
        copy = remote(buf.at[d - 1], all_ref.at[me, mine], as_.at[d - 1], ar.at[d - 1], peer)
        copy.start()
        first.append(copy)
    all_ref[me, mine, :] = rows_for(mf)
    fb_ref[mine, :] = feat_ref[...]
    for copy in first:
        copy.wait_recv()

    rows = all_ref.shape[1]
    chunk = rows // (2 * CUTS)

    def step_copy(d, s, q):
        block = blk_of(pos - s) if d == 0 else blk_of(pos + s)
        part = all_ref.at[block, pl.ds((d * CUTS + q) * chunk, chunk)]
        return remote(part, part, rs.at[d, s, q], rr.at[d, s, q], right if d == 0 else left)

    for q in range(CUTS):
        for d in range(2):
            step_copy(d, 0, q).start()
    later = []
    for d in range(1, nf):
        copy = remote(feat_ref, fb_ref.at[mine], fs.at[d - 1], fr.at[d - 1], peers[d - 1])
        copy.start()
        later.append(copy)

    def step(s, carry):
        for q in range(CUTS):
            for d in range(2):
                step_copy(d, s - 1, q).wait_recv()
                step_copy(d, s, q).start()
        return carry

    lax.fori_loop(1, n - 1, step, 0)
    for q in range(CUTS):
        for d in range(2):
            step_copy(d, n - 2, q).wait_recv()

    def drain(s, carry):
        for q in range(CUTS):
            for d in range(2):
                step_copy(d, s, q).wait_send()
        return carry

    lax.fori_loop(0, n - 1, drain, 0)
    for copy in later:
        copy.wait_recv()
    for copy in first + later:
        copy.wait_send()


def product_kernel(
    n, cap, tiles_row, idx, where, s_ref, own_ref, tiles_ref, sc_ref, cot_ref, out_ref, terms_ref, acc, gt
):
    step = pl.program_id(0)
    c = step % n
    first = c * cap
    tile = tiles_ref.shape[1]

    @pl.when((step == 0) | (step >= n))
    def _():
        acc[...] = jnp.zeros_like(acc)

    @pl.when(step < n)
    def _():
        for k in range(cap):
            col = pl.multiple_of(idx[2, first + k] * tile, tile)
            acc[idx[1, first + k]] += jnp.dot(
                tiles_ref[k], s_ref[0, pl.ds(col, tile), :], preferred_element_type=F32
            )

    @pl.when(step == n - 1)
    def _():
        for t in range(tiles_row):
            part = pl.ds(t * tile, tile)
            scale = sc_ref[part, :]
            v = scale * (acc[t] + own_ref[0, part, :].astype(F32))
            square = v * v
            th = jnp.tanh(GELU_C * (v + GELU_A * (square * v)))
            half = 0.5 * (1.0 + th)
            out_ref[part, :] = (v * half).astype(BF16)
            slope = half + 0.5 * v * (1.0 - th * th) * (GELU_C * (1.0 + 3.0 * GELU_A * square))
            grad = scale * (slope * cot_ref[part, :].astype(F32))
            gt[t] = grad.T.astype(BF16)

    @pl.when(step >= n)
    def _():
        for k in range(cap):
            acc[idx[3, first + k]] += jnp.dot(
                gt[idx[0, first + k]], tiles_ref[k], preferred_element_type=F32
            )
        own = jnp.where(c == where[0], 1.0, 0.0)
        for t in range(tiles_row):
            terms_ref[0, pl.ds(t * tile, tile), :] = (acc[t] + own * gt[t].astype(F32)).astype(BF16)


def scatter_kernel(
    n, nf, tile, factor, terms_ref, sct_ref, fb_ref, w_ref, gf_ref, gw_ref,
    land, hgt, hg, hg4, wbuf, wland, wsum, wfin, rs, rr, as_, ar, ws, wr, vs, vr,
):
    me, pos, blk_of = ring_of(n)
    mf = lax.axis_index("feat")
    right, left = (blk_of(pos + 1), mf), (blk_of(pos - 1), mf)
    fpeers = [(me, (mf + d) % nf) for d in range(1, nf)]
    bpeers = [((me + d) % n, mf) for d in range(1, n)]
    greet(fpeers + bpeers)
    rows = terms_ref.shape[1]
    chunk = rows // (2 * CUTS)

    def own_part(d, s, q):
        block = blk_of(pos - 1 - s) if d == 0 else blk_of(pos + 1 + s)
        return block, pl.ds((d * CUTS + q) * chunk, chunk)

    def step_copy(src, d, s, q):
        return remote(src, land.at[d, s, q], rs.at[d, s, q], rr.at[d, s, q], right if d == 0 else left)

    for q in range(CUTS):
        for d in range(2):
            step_copy(terms_ref.at[own_part(d, 0, q)], d, 0, q).start()

    def step(s, carry):
        for q in range(CUTS):
            for d in range(2):
                step_copy(land.at[d, s - 1, q], d, s - 1, q).wait_recv()
                block, part = own_part(d, s, q)
                summed = land[d, s - 1, q].astype(F32) + terms_ref[block, part, :].astype(F32)
                land[d, s - 1, q] = summed.astype(BF16)
                step_copy(land.at[d, s - 1, q], d, s, q).start()
        return carry

    lax.fori_loop(1, n - 1, step, 0)
    for q in range(CUTS):
        for d in range(2):
            step_copy(land.at[d, n - 2, q], d, n - 2, q).wait_recv()
            for t in range(chunk // tile):
                at = (d * CUTS + q) * chunk + t * tile
                total = land[d, n - 2, q, t * tile:(t + 1) * tile, :].astype(F32) + terms_ref[
                    me, at:at + tile, :
                ].astype(F32)
                total = total * sct_ref[at // tile][0:1, :]
                hgt[:, at:at + tile] = total.astype(BF16)
                hg[at:at + tile, :] = total.T.astype(BF16)

    quarter = rows // nf
    sent = []
    for d in (2, 3, 1):
        peer = fpeers[d - 1]
        src = hg.at[pl.ds(pl.multiple_of(peer[1] * quarter, quarter), quarter)]
        copy = remote(src, hg4.at[mf], as_.at[d - 1], ar.at[d - 1], peer)
        copy.start()
        sent.append(copy)
    hg4[mf] = hg[pl.ds(pl.multiple_of(mf * quarter, quarter), quarter), :]

    wgt = jnp.dot(hgt[...], fb_ref[...], preferred_element_type=F32)
    wbuf[...] = wgt.T.astype(BF16)
    piece = wsum.shape[0]

    def piece_of(b):
        return pl.ds(pl.multiple_of(b * piece, piece), piece)

    pieces = []
    for d in range(1, n):
        peer = bpeers[d - 1]
        copy = remote(wbuf.at[piece_of(peer[0])], wland.at[d - 1], ws.at[d - 1], wr.at[d - 1], peer)
        copy.start()
        pieces.append(copy)
    for copy in sent:
        copy.wait_recv()
    cols = hg.shape[1]
    total = None
    for f in range(nf):
        part = lax.dot_general(
            hg4[f], w_ref[:, f * cols:(f + 1) * cols], (((1,), (1,)), ((), ())),
            preferred_element_type=F32,
        )
        total = part if total is None else total + part
    gf_ref[...] = total.astype(BF16)
    summed = wbuf[piece_of(me), :].astype(F32)
    for d in range(1, n):
        pieces[d - 1].wait_recv()
        summed = summed + wland[d - 1].astype(F32)
    wsum[...] = summed.astype(BF16)
    finals = []
    for d in range(1, n):
        copy = remote(wsum, wfin.at[piece_of(me)], vs.at[d - 1], vr.at[d - 1], bpeers[d - 1])
        copy.start()
        finals.append(copy)
    wfin[piece_of(me), :] = wsum[...]

    def drain(s, carry):
        for q in range(CUTS):
            for d in range(2):
                step_copy(land.at[d, s, q], d, s, q).wait_send()
        return carry

    lax.fori_loop(0, n - 1, drain, 0)
    for copy in sent + pieces:
        copy.wait_send()
    for copy in finals:
        copy.wait_recv()
    gw_ref[...] = wfin[...].astype(F32) * factor
    for copy in finals:
        copy.wait_send()


def per_device(features, weight, tile_vals, pair_counts, slot_row, slot_col, cotangent):
    n = lax.axis_size("blk")
    nf = lax.axis_size("feat")
    tiles = tile_vals[0]
    slots, tile, _ = tiles.shape
    cap = slots // n
    rows, cols = cotangent.shape
    quarter, width = features.shape
    tiles_row = rows // tile
    filled = jnp.arange(slots) % cap < jnp.repeat(pair_counts[0], cap)
    row_ids, col_ids = slot_row[0], slot_col[0]
    idx = jnp.stack(
        [row_ids, jnp.where(filled, row_ids, tiles_row), col_ids, jnp.where(filled, col_ids, tiles_row)]
    ).astype(jnp.int32)
    where = jnp.full((1,), lax.axis_index("blk"), jnp.int32)
    dma = pltpu.SemaphoreType.DMA
    local = functools.partial(
        pltpu.CompilerParams, dimension_semantics=("arbitrary",), vmem_limit_bytes=LIMIT
    )

    sc, sct = pl.pallas_call(
        functools.partial(scaling_kernel, n, cap, tiles_row),
        grid_spec=pltpu.PrefetchScalarGridSpec(
            num_scalar_prefetch=1,
            grid=(n,),
            in_specs=[pl.BlockSpec((cap, tile, tile), lambda i, r: (i, 0, 0))],
            out_specs=[
                pl.BlockSpec((tiles_row, tile, tile), lambda i, r: (0, 0, 0)),
                pl.BlockSpec((tiles_row, 8, tile), lambda i, r: (0, 0, 0)),
            ],
            scratch_shapes=[pltpu.VMEM((tiles_row + 1, tile, tile), F32)],
        ),
        out_shape=[
            jax.ShapeDtypeStruct((tiles_row, tile, tile), F32),
            jax.ShapeDtypeStruct((tiles_row, 8, tile), F32),
        ],
        compiler_params=local(),
        name="scaling",
    )(idx[1], tiles)
    sc = sc.reshape(rows, tile)

    gathered, fblock = pl.pallas_call(
        functools.partial(gather_kernel, n, nf),
        out_shape=[
            jax.ShapeDtypeStruct((n, rows, cols), BF16),
            jax.ShapeDtypeStruct((rows, width), BF16),
        ],
        in_specs=[VMEM] * 3,
        out_specs=[VMEM] * 2,
        scratch_shapes=[
            pltpu.VMEM((nf - 1, quarter, cols), BF16),
            dma((nf - 1,)), dma((nf - 1,)), dma((nf - 1,)), dma((nf - 1,)),
            dma((2, n - 1, CUTS)), dma((2, n - 1, CUTS)),
        ],
        compiler_params=pltpu.CompilerParams(
            collective_id=0, has_side_effects=True, vmem_limit_bytes=LIMIT
        ),
        name="gather",
    )(features, weight, sc)

    output, terms = pl.pallas_call(
        functools.partial(product_kernel, n, cap, tiles_row),
        grid_spec=pltpu.PrefetchScalarGridSpec(
            num_scalar_prefetch=2,
            grid=(2 * n,),
            in_specs=[
                pl.BlockSpec((1, rows, cols), lambda i, r, w: (jnp.minimum(i, n - 1), 0, 0)),
                pl.BlockSpec((1, rows, cols), lambda i, r, w: (w[0], 0, 0)),
                pl.BlockSpec((cap, tile, tile), lambda i, r, w: (i % n, 0, 0)),
                pl.BlockSpec((rows, cols), lambda i, r, w: (0, 0)),
                pl.BlockSpec((rows, cols), lambda i, r, w: (0, 0)),
            ],
            out_specs=[
                pl.BlockSpec((rows, cols), lambda i, r, w: (0, 0)),
                pl.BlockSpec((1, rows, cols), lambda i, r, w: (jnp.maximum(i - n, 0), 0, 0)),
            ],
            scratch_shapes=[
                pltpu.VMEM((tiles_row + 1, tile, cols), F32),
                pltpu.VMEM((tiles_row, cols, tile), BF16),
            ],
        ),
        out_shape=[
            jax.ShapeDtypeStruct((rows, cols), BF16),
            jax.ShapeDtypeStruct((n, rows, cols), BF16),
        ],
        compiler_params=local(),
        name="products",
    )(idx, where, gathered, gathered, tiles, sc, cotangent)

    chunk = rows // (2 * CUTS)
    grad_features, grad_weight = pl.pallas_call(
        functools.partial(scatter_kernel, n, nf, tile, (rows * n) ** (-0.5)),
        out_shape=[
            jax.ShapeDtypeStruct((quarter, width), BF16),
            jax.ShapeDtypeStruct((width, cols), F32),
        ],
        in_specs=[VMEM] * 4,
        out_specs=[VMEM] * 2,
        scratch_shapes=[
            pltpu.VMEM((2, n - 1, CUTS, chunk, cols), BF16),
            pltpu.VMEM((cols, rows), BF16),
            pltpu.VMEM((rows, cols), BF16),
            pltpu.VMEM((nf, quarter, cols), BF16),
            pltpu.VMEM((width, cols), BF16),
            pltpu.VMEM((n - 1, width // n, cols), BF16),
            pltpu.VMEM((width // n, cols), BF16),
            pltpu.VMEM((width, cols), BF16),
            dma((2, n - 1, CUTS)), dma((2, n - 1, CUTS)),
            dma((nf - 1,)), dma((nf - 1,)),
            dma((n - 1,)), dma((n - 1,)), dma((n - 1,)), dma((n - 1,)),
        ],
        compiler_params=pltpu.CompilerParams(
            collective_id=1, has_side_effects=True, vmem_limit_bytes=LIMIT
        ),
        name="scatter",
    )(terms, sct, fblock, weight)
    return (output, grad_features, grad_weight)


def solution(mesh):
    in_specs = (
        P(("blk", "feat"), None),
        P(),
        P("blk", None, None, None),
        P("blk", None),
        P("blk", None),
        P("blk", None),
        P("blk", "feat"),
    )
    out_specs = (P("blk", "feat"), P(("blk", "feat"), None), P(None, "feat"))
    return jax.shard_map(
        per_device, mesh=mesh, in_specs=in_specs, out_specs=out_specs, check_vma=False
    )
```

```python
import functools

import jax
import jax.numpy as jnp
from jax import lax
from jax.experimental import pallas as pl
from jax.experimental.pallas import tpu as pltpu
from jax.sharding import PartitionSpec as P

MESH = pl.DeviceIdType.MESH
VMEM = pl.BlockSpec(memory_space=pltpu.VMEM)
F32, BF16 = jnp.float32, jnp.bfloat16
LIMIT = 56 * 1024 * 1024
CUTS = 2
GELU_C = 0.7978845608028654
GELU_A = 0.044715


def ring_of(n):
    me = lax.axis_index("blk")
    half = n // 2
    pos = jnp.where(me % 2 == 0, me // 2, n - 1 - me // 2)

    def blk_of(p):
        p = (p + 2 * n) % n
        return jnp.where(p < half, 2 * p, 2 * (n - 1 - p) + 1)

    return me, pos, blk_of


def greet(peers):
    barrier = pltpu.get_barrier_semaphore()
    for peer in peers:
        pl.semaphore_signal(barrier, inc=1, device_id=peer, device_id_type=MESH)
    pl.semaphore_wait(barrier, len(peers))


def remote(src, dst, send, recv, peer):
    return pltpu.make_async_remote_copy(
        src_ref=src, dst_ref=dst, send_sem=send, recv_sem=recv, device_id=peer, device_id_type=MESH
    )


def dense_kernel(n, cap, tiles_row, cnt_ref, row_ref, col_ref, tiles_ref, dense_ref, sc_ref, sct_ref, acc):
    c = pl.program_id(0)
    tile = tiles_ref.shape[1]
    across = tiles_row // 2

    @pl.when(c == 0)
    def _():
        acc[...] = jnp.zeros_like(acc)

    dense_ref[...] = jnp.zeros_like(dense_ref)
    count = cnt_ref[0, c]
    for k in range(cap):

        @pl.when(k < count)
        def _():
            row, col = row_ref[0, c * cap + k], col_ref[0, c * cap + k]
            value = tiles_ref[k]
            acc[row] += value.astype(F32)
            rows_at = pl.ds(pl.multiple_of(row * tile, tile), tile)
            cols_at = pl.ds(pl.multiple_of(col % across * tile, tile), tile)
            dense_ref[0, col // across, rows_at, cols_at] += value

    @pl.when(c == n - 1)
    def _():
        for t in range(tiles_row):
            degree = 1.0 + jnp.sum(acc[t], axis=1, keepdims=True)
            wide = jnp.broadcast_to(lax.rsqrt(degree), acc.shape[1:])
            sc_ref[t * tile:(t + 1) * tile, :] = wide
            sct_ref[:, t * tile:(t + 1) * tile] = wide.T[0:8]


def layer_kernel(
    n, nf, tile, feat_ref, w_ref, sc_ref, sct_ref, cot_ref, dense_ref, out_ref, gf_ref, wfin,
    all_ref, fb_ref, buf, abuf, acc, gt, stage, tbuf, land, hgt, hg, hg4, wbuf, wland, wsum,
    asem, s1, r1, s2, r2, s3, r3, s4, r4, s5, r5, s6, r6, s7, r7,
):
    me, pos, blk_of = ring_of(n)
    mf = lax.axis_index("feat")
    quarter = feat_ref.shape[0]
    rows, cols = all_ref.shape[1:]
    half = rows // 2
    right, left = (blk_of(pos + 1), mf), (blk_of(pos - 1), mf)
    fpeers = [(me, (mf + d) % nf) for d in range(1, nf)]
    bpeers = [((me + d) % n, mf) for d in range(1, n)]
    greet(fpeers + bpeers)

    def block_of(d, u):
        return blk_of(pos - u) if d == 0 else blk_of(pos + u)

    def fetch(d, v):
        u = jnp.where(v < n, v, v - n + 1)
        slot = v % 2
        return pltpu.make_async_copy(dense_ref.at[block_of(d, u), d], abuf.at[slot, d], asem.at[slot, d])

    def begin(v):
        for d in range(2):
            fetch(d, v).start()

    begin(0)
    mine = pl.ds(pl.multiple_of(mf * quarter, quarter), quarter)
    scale = sc_ref[mine, :]

    def rows_for(f):
        w = w_ref[:, pl.ds(pl.multiple_of(f * cols, cols), cols)]
        h = jnp.dot(feat_ref[...], w, preferred_element_type=F32)
        return (scale * h).astype(BF16)

    first = []
    for d in (2, 3, 1):
        peer = fpeers[d - 1]
        buf[d - 1] = rows_for(peer[1])
        copy = remote(buf.at[d - 1], all_ref.at[me, mine], s1.at[d - 1], r1.at[d - 1], peer)
        copy.start()
        first.append(copy)
    all_ref[me, mine, :] = rows_for(mf)
    fb_ref[mine, :] = feat_ref[...]
    for copy in first:
        copy.wait_recv()

    chunk = half // CUTS

    def gather_copy(d, s, q):
        part = all_ref.at[block_of(d, s), pl.ds(d * half + q * chunk, chunk)]
        return remote(part, part, s2.at[d, s, q], r2.at[d, s, q], right if d == 0 else left)

    for q in range(CUTS):
        for d in range(2):
            gather_copy(d, 0, q).start()
    later = []
    for d in range(1, nf):
        copy = remote(feat_ref, fb_ref.at[mine], s3.at[d - 1], r3.at[d - 1], fpeers[d - 1])
        copy.start()
        later.append(copy)

    def fold(v):
        begin(v + 1)
        for d in range(2):
            fetch(d, v).wait()
            acc[...] += jnp.dot(
                abuf[v % 2, d],
                all_ref[block_of(d, v), d * half:(d + 1) * half, :],
                preferred_element_type=F32,
            )

    acc[...] = all_ref[me].astype(F32)
    fold(0)

    def gather_step(s, carry):
        for q in range(CUTS):
            for d in range(2):
                gather_copy(d, s - 1, q).wait_recv()
                gather_copy(d, s, q).start()
        fold(s)
        return carry

    lax.fori_loop(1, n - 1, gather_step, 0)
    for q in range(CUTS):
        for d in range(2):
            gather_copy(d, n - 2, q).wait_recv()
    fold(n - 1)

    for t in range(rows // tile):
        part = slice(t * tile, (t + 1) * tile)
        scale = sc_ref[part, :]
        v = scale * acc[part, :]
        square = v * v
        th = jnp.tanh(GELU_C * (v + GELU_A * (square * v)))
        level = 0.5 * (1.0 + th)
        out_ref[part, :] = (v * level).astype(BF16)
        slope = level + 0.5 * v * (1.0 - th * th) * (GELU_C * (1.0 + 3.0 * GELU_A * square))
        gt[:, part] = (scale * (slope * cot_ref[part, :].astype(F32))).T.astype(BF16)

    strip = cols // CUTS

    def scatter_copy(src, d, s, q):
        return remote(src, land.at[d, s, q], s4.at[d, s, q], r4.at[d, s, q], right if d == 0 else left)

    def term(v, d):
        fetch(d, v).wait()
        return jnp.dot(gt[...], abuf[v % 2, d], preferred_element_type=F32)

    begin(n + 1)
    for d in range(2):
        value = term(n, d).astype(BF16)
        for q in range(CUTS):
            stage[d, q] = value[q * strip:(q + 1) * strip]
            scatter_copy(stage.at[d, q], d, 0, q).start()

    def scatter_step(s, carry):
        begin(n + s + 1)
        for d in range(2):
            tbuf[d] = term(n + s, d)
        for q in range(CUTS):
            for d in range(2):
                slot = land.at[d, s - 1, q]
                scatter_copy(slot, d, s - 1, q).wait_recv()
                slot[...] = (slot[...].astype(F32) + tbuf[d, q * strip:(q + 1) * strip, :]).astype(BF16)
                scatter_copy(slot, d, s, q).start()
        return carry

    lax.fori_loop(1, n - 1, scatter_step, 0)
    for d in range(2):
        tbuf[d] = term(2 * n - 1, d) + gt[:, d * half:(d + 1) * half].astype(F32)
    for q in range(CUTS):
        for d in range(2):
            slot = land.at[d, n - 2, q]
            scatter_copy(slot, d, n - 2, q).wait_recv()
            part = slice(d * half, (d + 1) * half)
            total = slot[...].astype(F32) + tbuf[d, q * strip:(q + 1) * strip, :]
            tbuf[d, q * strip:(q + 1) * strip, :] = total * sct_ref[0:1, part]
    for t in range(rows // tile):
        d, at = t * tile // half, t * tile % half
        total = tbuf[d, :, at:at + tile]
        hgt[:, t * tile:(t + 1) * tile] = total.astype(BF16)
        hg[t * tile:(t + 1) * tile, :] = total.T.astype(BF16)

    sent = []
    for d in (2, 3, 1):
        peer = fpeers[d - 1]
        src = hg.at[pl.ds(pl.multiple_of(peer[1] * quarter, quarter), quarter)]
        copy = remote(src, hg4.at[mf], s5.at[d - 1], r5.at[d - 1], peer)
        copy.start()
        sent.append(copy)
    hg4[mf] = hg[mine, :]
    for copy in later:
        copy.wait_recv()
    wgt = jnp.dot(hgt[...], fb_ref[...], preferred_element_type=F32)
    wbuf[...] = wgt.T.astype(BF16)
    piece = wsum.shape[0]

    def piece_of(b):
        return pl.ds(pl.multiple_of(b * piece, piece), piece)

    pieces = []
    for d in range(1, n):
        peer = bpeers[d - 1]
        copy = remote(wbuf.at[piece_of(peer[0])], wland.at[d - 1], s6.at[d - 1], r6.at[d - 1], peer)
        copy.start()
        pieces.append(copy)
    summed = wbuf[piece_of(me), :].astype(F32)
    for d in range(1, n):
        pieces[d - 1].wait_recv()
        summed = summed + wland[d - 1].astype(F32)
    wsum[...] = summed.astype(BF16)
    finals = []
    for d in range(1, n):
        copy = remote(wsum, wfin.at[piece_of(me)], s7.at[d - 1], r7.at[d - 1], bpeers[d - 1])
        copy.start()
        finals.append(copy)
    wfin[piece_of(me), :] = wsum[...]
    for copy in sent:
        copy.wait_recv()
    total = None
    for f in range(nf):
        part = lax.dot_general(
            hg4[f], w_ref[:, f * cols:(f + 1) * cols], (((1,), (1,)), ((), ())),
            preferred_element_type=F32,
        )
        total = part if total is None else total + part
    gf_ref[...] = total.astype(BF16)

    def drain(s, carry):
        for q in range(CUTS):
            for d in range(2):
                gather_copy(d, s, q).wait_send()
                scatter_copy(land.at[d, s, q], d, s, q).wait_send()
        return carry

    lax.fori_loop(0, n - 1, drain, 0)
    for copy in first + later + sent + pieces:
        copy.wait_send()
    for copy in finals:
        copy.wait_recv()
    for copy in finals:
        copy.wait_send()


def finish_kernel(factor, out_in, gf_in, w_in, out_ref, gf_ref, gw_ref):
    out_ref[...] = out_in[...]
    gf_ref[...] = gf_in[...]
    gw_ref[...] = w_in[...].astype(F32) * factor


def per_device(features, weight, tile_vals, pair_counts, slot_row, slot_col, cotangent):
    n = lax.axis_size("blk")
    nf = lax.axis_size("feat")
    tiles = tile_vals[0]
    slots, tile, _ = tiles.shape
    cap = slots // n
    rows, cols = cotangent.shape
    quarter, width = features.shape
    tiles_row = rows // tile
    half = rows // 2
    dma = pltpu.SemaphoreType.DMA
    shape = jax.ShapeDtypeStruct

    dense, sc, sct = pl.pallas_call(
        functools.partial(dense_kernel, n, cap, tiles_row),
        grid_spec=pltpu.PrefetchScalarGridSpec(
            num_scalar_prefetch=3,
            grid=(n,),
            in_specs=[pl.BlockSpec((cap, tile, tile), lambda i, *_: (i, 0, 0))],
            out_specs=[
                pl.BlockSpec((1, 2, rows, half), lambda i, *_: (i, 0, 0, 0)),
                pl.BlockSpec((rows, tile), lambda i, *_: (0, 0)),
                pl.BlockSpec((8, rows), lambda i, *_: (0, 0)),
            ],
            scratch_shapes=[pltpu.VMEM((tiles_row, tile, tile), F32)],
        ),
        out_shape=[shape((n, 2, rows, half), BF16), shape((rows, tile), F32), shape((8, rows), F32)],
        compiler_params=pltpu.CompilerParams(
            dimension_semantics=("arbitrary",), vmem_limit_bytes=LIMIT
        ),
        name="dense",
    )(pair_counts, slot_row, slot_col, tiles)

    ring = dma((2, n - 1, CUTS))
    peers, others = dma((nf - 1,)), dma((n - 1,))
    vmem = pltpu.VMEM
    output, grad_features, summed = pl.pallas_call(
        functools.partial(layer_kernel, n, nf, tile),
        out_shape=[shape((rows, cols), BF16), shape((quarter, width), BF16), shape((width, cols), BF16)],
        in_specs=[VMEM] * 5 + [pl.BlockSpec(memory_space=pl.ANY)],
        out_specs=[VMEM] * 3,
        scratch_shapes=[
            vmem((n, rows, cols), BF16),
            vmem((rows, width), BF16),
            vmem((nf - 1, quarter, cols), BF16),
            vmem((2, 2, rows, half), BF16),
            vmem((rows, cols), F32),
            vmem((cols, rows), BF16),
            vmem((2, CUTS, cols // CUTS, half), BF16),
            vmem((2, cols, half), F32),
            vmem((2, n - 1, CUTS, cols // CUTS, half), BF16),
            vmem((cols, rows), BF16),
            vmem((rows, cols), BF16),
            vmem((nf, quarter, cols), BF16),
            vmem((width, cols), BF16),
            vmem((n - 1, width // n, cols), BF16),
            vmem((width // n, cols), BF16),
            dma((2, 2)),
            peers, peers, ring, ring, peers, peers, ring, ring, peers, peers,
            others, others, others, others,
        ],
        compiler_params=pltpu.CompilerParams(
            collective_id=0, has_side_effects=True, vmem_limit_bytes=LIMIT
        ),
        name="layer",
    )(features, weight, sc, sct, cotangent, dense)

    return tuple(
        pl.pallas_call(
            functools.partial(finish_kernel, (rows * n) ** (-0.5)),
            out_shape=[shape((rows, cols), BF16), shape((quarter, width), BF16), shape((width, cols), F32)],
            in_specs=[VMEM] * 3,
            out_specs=[VMEM] * 3,
            name="finish",
        )(output, grad_features, summed)
    )


def solution(mesh):
    in_specs = (
        P(("blk", "feat"), None),
        P(),
        P("blk", None, None, None),
        P("blk", None),
        P("blk", None),
        P("blk", None),
        P("blk", "feat"),
    )
    out_specs = (P("blk", "feat"), P(("blk", "feat"), None), P(None, "feat"))
    return jax.shard_map(
        per_device, mesh=mesh, in_specs=in_specs, out_specs=out_specs, check_vma=False
    )
```

```python
import functools

import jax
import jax.numpy as jnp
from jax import lax
from jax.experimental import pallas as pl
from jax.experimental.pallas import tpu as pltpu
from jax.sharding import PartitionSpec as P

MESH = pl.DeviceIdType.MESH
VMEM = pl.BlockSpec(memory_space=pltpu.VMEM)
F32, BF16 = jnp.float32, jnp.bfloat16
LIMIT = 56 * 1024 * 1024
CUTS = 4
GELU_C = 0.7978845608028654
GELU_A = 0.044715


def ring_of(n):
    me = lax.axis_index("blk")
    half = n // 2
    pos = jnp.where(me % 2 == 0, me // 2, n - 1 - me // 2)

    def blk_of(p):
        p = (p + 2 * n) % n
        return jnp.where(p < half, 2 * p, 2 * (n - 1 - p) + 1)

    return me, pos, blk_of


def greet(peers):
    barrier = pltpu.get_barrier_semaphore()
    for peer in peers:
        pl.semaphore_signal(barrier, inc=1, device_id=peer, device_id_type=MESH)
    pl.semaphore_wait(barrier, len(peers))


def remote(src, dst, send, recv, peer):
    return pltpu.make_async_remote_copy(
        src_ref=src, dst_ref=dst, send_sem=send, recv_sem=recv, device_id=peer, device_id_type=MESH
    )


def dense_kernel(n, cap, tiles_row, cnt_ref, row_ref, col_ref, tiles_ref, dense_ref, sc_ref, sct_ref, acc):
    c = pl.program_id(0)
    tile = tiles_ref.shape[1]
    across = tiles_row // 2

    @pl.when(c == 0)
    def _():
        acc[...] = jnp.zeros_like(acc)

    dense_ref[...] = jnp.zeros_like(dense_ref)
    count = cnt_ref[0, c]
    for k in range(cap):

        @pl.when(k < count)
        def _():
            row, col = row_ref[0, c * cap + k], col_ref[0, c * cap + k]
            value = tiles_ref[k]
            acc[row] += value.astype(F32)
            rows_at = pl.ds(pl.multiple_of(row * tile, tile), tile)
            cols_at = pl.ds(pl.multiple_of(col % across * tile, tile), tile)
            dense_ref[0, col // across, rows_at, cols_at] += value

    @pl.when(c == n - 1)
    def _():
        for t in range(tiles_row):
            degree = 1.0 + jnp.sum(acc[t], axis=1, keepdims=True)
            wide = jnp.broadcast_to(lax.rsqrt(degree), acc.shape[1:])
            sc_ref[t * tile:(t + 1) * tile, :] = wide
            sct_ref[:, t * tile:(t + 1) * tile] = wide.T[0:8]


def layer_kernel(
    n, nf, tile, feat_ref, w_ref, sc_ref, sct_ref, cot_ref, dense_ref, out_ref, gf_ref, wfin,
    all_ref, fb_ref, buf, abuf, acc, gt, stage, tbuf, land, hgt, hg, hg4, wbuf, wland, wsum,
    asem, s1, r1, s2, r2, s3, r3, s4, r4, s5, r5, s6, r6, s7, r7,
):
    me, pos, blk_of = ring_of(n)
    mf = lax.axis_index("feat")
    quarter = feat_ref.shape[0]
    rows, cols = all_ref.shape[1:]
    half = rows // 2
    right, left = (blk_of(pos + 1), mf), (blk_of(pos - 1), mf)
    fpeers = [(me, (mf + d) % nf) for d in range(1, nf)]
    bpeers = [((me + d) % n, mf) for d in range(1, n)]
    greet(fpeers + bpeers)

    def block_of(d, u):
        return blk_of(pos - u) if d == 0 else blk_of(pos + u)

    def fetch(d, v):
        u = jnp.where(v < n, v, v - n + 1)
        slot = v % 2
        return pltpu.make_async_copy(dense_ref.at[block_of(d, u), d], abuf.at[slot, d], asem.at[slot, d])

    def begin(v):
        for d in range(2):
            fetch(d, v).start()

    begin(0)
    mine = pl.ds(pl.multiple_of(mf * quarter, quarter), quarter)
    scale = sc_ref[mine, :]

    def rows_for(f):
        w = w_ref[:, pl.ds(pl.multiple_of(f * cols, cols), cols)]
        h = jnp.dot(feat_ref[...], w, preferred_element_type=F32)
        return (scale * h).astype(BF16)

    first = []
    for d in (2, 3, 1):
        peer = fpeers[d - 1]
        buf[d - 1] = rows_for(peer[1])
        copy = remote(buf.at[d - 1], all_ref.at[me, mine], s1.at[d - 1], r1.at[d - 1], peer)
        copy.start()
        first.append(copy)
    all_ref[me, mine, :] = rows_for(mf)
    fb_ref[mine, :] = feat_ref[...]
    for copy in first:
        copy.wait_recv()

    chunk = half // CUTS

    def gather_copy(d, s, q):
        part = all_ref.at[block_of(d, s), pl.ds(d * half + q * chunk, chunk)]
        return remote(part, part, s2.at[d, s, q], r2.at[d, s, q], right if d == 0 else left)

    for q in range(CUTS):
        for d in range(2):
            gather_copy(d, 0, q).start()
    later = []
    for d in range(1, nf):
        copy = remote(feat_ref, fb_ref.at[mine], s3.at[d - 1], r3.at[d - 1], fpeers[d - 1])
        copy.start()
        later.append(copy)

    def fold(v):
        begin(v + 1)
        for d in range(2):
            fetch(d, v).wait()
            acc[...] += jnp.dot(
                abuf[v % 2, d],
                all_ref[block_of(d, v), d * half:(d + 1) * half, :],
                preferred_element_type=F32,
            )

    acc[...] = all_ref[me].astype(F32)
    fold(0)

    def gather_step(s, carry):
        for q in range(CUTS):
            for d in range(2):
                gather_copy(d, s - 1, q).wait_recv()
                gather_copy(d, s, q).start()
        fold(s)
        return carry

    lax.fori_loop(1, n - 1, gather_step, 0)
    for q in range(CUTS):
        for d in range(2):
            gather_copy(d, n - 2, q).wait_recv()
    fold(n - 1)

    for t in range(rows // tile):
        part = slice(t * tile, (t + 1) * tile)
        scale = sc_ref[part, :]
        v = scale * acc[part, :]
        square = v * v
        th = jnp.tanh(GELU_C * (v + GELU_A * (square * v)))
        level = 0.5 * (1.0 + th)
        out_ref[part, :] = (v * level).astype(BF16)
        slope = level + 0.5 * v * (1.0 - th * th) * (GELU_C * (1.0 + 3.0 * GELU_A * square))
        gt[:, part] = (scale * (slope * cot_ref[part, :].astype(F32))).T.astype(BF16)

    strip = cols // CUTS

    def scatter_copy(src, d, s, q):
        return remote(src, land.at[d, s, q], s4.at[d, s, q], r4.at[d, s, q], right if d == 0 else left)

    def term(v, d):
        fetch(d, v).wait()
        return jnp.dot(gt[...], abuf[v % 2, d], preferred_element_type=F32)

    begin(n + 1)
    for d in range(2):
        value = term(n, d).astype(BF16)
        for q in range(CUTS):
            stage[d, q] = value[q * strip:(q + 1) * strip]
            scatter_copy(stage.at[d, q], d, 0, q).start()

    def scatter_step(s, carry):
        begin(n + s + 1)
        for d in range(2):
            tbuf[d] = term(n + s, d)
        for q in range(CUTS):
            for d in range(2):
                slot = land.at[d, s - 1, q]
                scatter_copy(slot, d, s - 1, q).wait_recv()
                slot[...] = (slot[...].astype(F32) + tbuf[d, q * strip:(q + 1) * strip, :]).astype(BF16)
                scatter_copy(slot, d, s, q).start()
        return carry

    lax.fori_loop(1, n - 1, scatter_step, 0)
    for d in range(2):
        tbuf[d] = term(2 * n - 1, d) + gt[:, d * half:(d + 1) * half].astype(F32)
    for q in range(CUTS):
        for d in range(2):
            slot = land.at[d, n - 2, q]
            scatter_copy(slot, d, n - 2, q).wait_recv()
            part = slice(d * half, (d + 1) * half)
            total = slot[...].astype(F32) + tbuf[d, q * strip:(q + 1) * strip, :]
            tbuf[d, q * strip:(q + 1) * strip, :] = total * sct_ref[0:1, part]
    for t in range(rows // tile):
        d, at = t * tile // half, t * tile % half
        total = tbuf[d, :, at:at + tile]
        hgt[:, t * tile:(t + 1) * tile] = total.astype(BF16)
        hg[t * tile:(t + 1) * tile, :] = total.T.astype(BF16)

    sent = []
    for d in (2, 3, 1):
        peer = fpeers[d - 1]
        src = hg.at[pl.ds(pl.multiple_of(peer[1] * quarter, quarter), quarter)]
        copy = remote(src, hg4.at[mf], s5.at[d - 1], r5.at[d - 1], peer)
        copy.start()
        sent.append(copy)
    hg4[mf] = hg[mine, :]
    for copy in later:
        copy.wait_recv()
    wgt = jnp.dot(hgt[...], fb_ref[...], preferred_element_type=F32)
    wbuf[...] = wgt.T.astype(BF16)
    piece = wsum.shape[0]

    def piece_of(b):
        return pl.ds(pl.multiple_of(b * piece, piece), piece)

    pieces = []
    for d in range(1, n):
        peer = bpeers[d - 1]
        copy = remote(wbuf.at[piece_of(peer[0])], wland.at[d - 1], s6.at[d - 1], r6.at[d - 1], peer)
        copy.start()
        pieces.append(copy)
    summed = wbuf[piece_of(me), :].astype(F32)
    for d in range(1, n):
        pieces[d - 1].wait_recv()
        summed = summed + wland[d - 1].astype(F32)
    wsum[...] = summed.astype(BF16)
    finals = []
    for d in range(1, n):
        copy = remote(wsum, wfin.at[piece_of(me)], s7.at[d - 1], r7.at[d - 1], bpeers[d - 1])
        copy.start()
        finals.append(copy)
    wfin[piece_of(me), :] = wsum[...]
    for copy in sent:
        copy.wait_recv()
    total = None
    for f in range(nf):
        part = lax.dot_general(
            hg4[f], w_ref[:, f * cols:(f + 1) * cols], (((1,), (1,)), ((), ())),
            preferred_element_type=F32,
        )
        total = part if total is None else total + part
    gf_ref[...] = total.astype(BF16)

    def drain(s, carry):
        for q in range(CUTS):
            for d in range(2):
                gather_copy(d, s, q).wait_send()
                scatter_copy(land.at[d, s, q], d, s, q).wait_send()
        return carry

    lax.fori_loop(0, n - 1, drain, 0)
    for copy in first + later + sent + pieces:
        copy.wait_send()
    for copy in finals:
        copy.wait_recv()
    for copy in finals:
        copy.wait_send()


def finish_kernel(factor, out_in, gf_in, w_in, out_ref, gf_ref, gw_ref):
    out_ref[...] = out_in[...]
    gf_ref[...] = gf_in[...]
    gw_ref[...] = w_in[...].astype(F32) * factor


def per_device(features, weight, tile_vals, pair_counts, slot_row, slot_col, cotangent):
    n = lax.axis_size("blk")
    nf = lax.axis_size("feat")
    tiles = tile_vals[0]
    slots, tile, _ = tiles.shape
    cap = slots // n
    rows, cols = cotangent.shape
    quarter, width = features.shape
    tiles_row = rows // tile
    half = rows // 2
    dma = pltpu.SemaphoreType.DMA
    shape = jax.ShapeDtypeStruct

    dense, sc, sct = pl.pallas_call(
        functools.partial(dense_kernel, n, cap, tiles_row),
        grid_spec=pltpu.PrefetchScalarGridSpec(
            num_scalar_prefetch=3,
            grid=(n,),
            in_specs=[pl.BlockSpec((cap, tile, tile), lambda i, *_: (i, 0, 0))],
            out_specs=[
                pl.BlockSpec((1, 2, rows, half), lambda i, *_: (i, 0, 0, 0)),
                pl.BlockSpec((rows, tile), lambda i, *_: (0, 0)),
                pl.BlockSpec((8, rows), lambda i, *_: (0, 0)),
            ],
            scratch_shapes=[pltpu.VMEM((tiles_row, tile, tile), F32)],
        ),
        out_shape=[shape((n, 2, rows, half), BF16), shape((rows, tile), F32), shape((8, rows), F32)],
        compiler_params=pltpu.CompilerParams(
            dimension_semantics=("arbitrary",), vmem_limit_bytes=LIMIT
        ),
        name="dense",
    )(pair_counts, slot_row, slot_col, tiles)

    ring = dma((2, n - 1, CUTS))
    peers, others = dma((nf - 1,)), dma((n - 1,))
    vmem = pltpu.VMEM
    output, grad_features, summed = pl.pallas_call(
        functools.partial(layer_kernel, n, nf, tile),
        out_shape=[shape((rows, cols), BF16), shape((quarter, width), BF16), shape((width, cols), BF16)],
        in_specs=[VMEM] * 5 + [pl.BlockSpec(memory_space=pl.ANY)],
        out_specs=[VMEM] * 3,
        scratch_shapes=[
            vmem((n, rows, cols), BF16),
            vmem((rows, width), BF16),
            vmem((nf - 1, quarter, cols), BF16),
            vmem((2, 2, rows, half), BF16),
            vmem((rows, cols), F32),
            vmem((cols, rows), BF16),
            vmem((2, CUTS, cols // CUTS, half), BF16),
            vmem((2, cols, half), F32),
            vmem((2, n - 1, CUTS, cols // CUTS, half), BF16),
            vmem((cols, rows), BF16),
            vmem((rows, cols), BF16),
            vmem((nf, quarter, cols), BF16),
            vmem((width, cols), BF16),
            vmem((n - 1, width // n, cols), BF16),
            vmem((width // n, cols), BF16),
            dma((2, 2)),
            peers, peers, ring, ring, peers, peers, ring, ring, peers, peers,
            others, others, others, others,
        ],
        compiler_params=pltpu.CompilerParams(
            collective_id=0, has_side_effects=True, vmem_limit_bytes=LIMIT
        ),
        name="layer",
    )(features, weight, sc, sct, cotangent, dense)

    return tuple(
        pl.pallas_call(
            functools.partial(finish_kernel, (rows * n) ** (-0.5)),
            out_shape=[shape((rows, cols), BF16), shape((quarter, width), BF16), shape((width, cols), F32)],
            in_specs=[VMEM] * 3,
            out_specs=[VMEM] * 3,
            name="finish",
        )(output, grad_features, summed)
    )


def solution(mesh):
    in_specs = (
        P(("blk", "feat"), None),
        P(),
        P("blk", None, None, None),
        P("blk", None),
        P("blk", None),
        P("blk", None),
        P("blk", "feat"),
    )
    out_specs = (P("blk", "feat"), P(("blk", "feat"), None), P(None, "feat"))
    return jax.shard_map(
        per_device, mesh=mesh, in_specs=in_specs, out_specs=out_specs, check_vma=False
    )
```

```python
import functools

import jax
import jax.numpy as jnp
from jax import lax
from jax.experimental import pallas as pl
from jax.experimental.pallas import tpu as pltpu
from jax.sharding import PartitionSpec as P

MESH = pl.DeviceIdType.MESH
VMEM = pl.BlockSpec(memory_space=pltpu.VMEM)
F32, BF16 = jnp.float32, jnp.bfloat16
LIMIT = 56 * 1024 * 1024
CUTS = 8
GELU_C = 0.7978845608028654
GELU_A = 0.044715


def ring_of(n):
    me = lax.axis_index("blk")
    half = n // 2
    pos = jnp.where(me % 2 == 0, me // 2, n - 1 - me // 2)

    def blk_of(p):
        p = (p + 2 * n) % n
        return jnp.where(p < half, 2 * p, 2 * (n - 1 - p) + 1)

    return me, pos, blk_of


def greet(peers):
    barrier = pltpu.get_barrier_semaphore()
    for peer in peers:
        pl.semaphore_signal(barrier, inc=1, device_id=peer, device_id_type=MESH)
    pl.semaphore_wait(barrier, len(peers))


def remote(src, dst, send, recv, peer):
    return pltpu.make_async_remote_copy(
        src_ref=src, dst_ref=dst, send_sem=send, recv_sem=recv, device_id=peer, device_id_type=MESH
    )


def dense_kernel(n, cap, tiles_row, cnt_ref, row_ref, col_ref, tiles_ref, dense_ref, sc_ref, sct_ref, acc):
    c = pl.program_id(0)
    tile = tiles_ref.shape[1]
    across = tiles_row // 2

    @pl.when(c == 0)
    def _():
        acc[...] = jnp.zeros_like(acc)

    dense_ref[...] = jnp.zeros_like(dense_ref)
    count = cnt_ref[0, c]
    for k in range(cap):

        @pl.when(k < count)
        def _():
            row, col = row_ref[0, c * cap + k], col_ref[0, c * cap + k]
            value = tiles_ref[k]
            acc[row] += value.astype(F32)
            rows_at = pl.ds(pl.multiple_of(row * tile, tile), tile)
            cols_at = pl.ds(pl.multiple_of(col % across * tile, tile), tile)
            dense_ref[0, col // across, rows_at, cols_at] += value

    @pl.when(c == n - 1)
    def _():
        for t in range(tiles_row):
            degree = 1.0 + jnp.sum(acc[t], axis=1, keepdims=True)
            wide = jnp.broadcast_to(lax.rsqrt(degree), acc.shape[1:])
            sc_ref[t * tile:(t + 1) * tile, :] = wide
            sct_ref[:, t * tile:(t + 1) * tile] = wide.T[0:8]


def layer_kernel(
    n, nf, tile, feat_ref, w_ref, sc_ref, sct_ref, cot_ref, dense_ref, out_ref, gf_ref, wfin,
    all_ref, fb_ref, buf, abuf, acc, gt, stage, tbuf, land, hgt, hg, hg4, wbuf, wland, wsum,
    asem, s1, r1, s2, r2, s3, r3, s4, r4, s5, r5, s6, r6, s7, r7,
):
    me, pos, blk_of = ring_of(n)
    mf = lax.axis_index("feat")
    quarter = feat_ref.shape[0]
    rows, cols = all_ref.shape[1:]
    half = rows // 2
    right, left = (blk_of(pos + 1), mf), (blk_of(pos - 1), mf)
    fpeers = [(me, (mf + d) % nf) for d in range(1, nf)]
    bpeers = [((me + d) % n, mf) for d in range(1, n)]
    greet(fpeers + bpeers)

    def block_of(d, u):
        return blk_of(pos - u) if d == 0 else blk_of(pos + u)

    def fetch(d, v):
        u = jnp.where(v < n, v, v - n + 1)
        slot = v % 2
        return pltpu.make_async_copy(dense_ref.at[block_of(d, u), d], abuf.at[slot, d], asem.at[slot, d])

    def begin(v):
        for d in range(2):
            fetch(d, v).start()

    begin(0)
    mine = pl.ds(pl.multiple_of(mf * quarter, quarter), quarter)
    scale = sc_ref[mine, :]

    def rows_for(f):
        w = w_ref[:, pl.ds(pl.multiple_of(f * cols, cols), cols)]
        h = jnp.dot(feat_ref[...], w, preferred_element_type=F32)
        return (scale * h).astype(BF16)

    first = []
    for d in (2, 3, 1):
        peer = fpeers[d - 1]
        buf[d - 1] = rows_for(peer[1])
        copy = remote(buf.at[d - 1], all_ref.at[me, mine], s1.at[d - 1], r1.at[d - 1], peer)
        copy.start()
        first.append(copy)
    all_ref[me, mine, :] = rows_for(mf)
    fb_ref[mine, :] = feat_ref[...]
    for copy in first:
        copy.wait_recv()

    chunk = half // CUTS

    def gather_copy(d, s, q):
        part = all_ref.at[block_of(d, s), pl.ds(d * half + q * chunk, chunk)]
        return remote(part, part, s2.at[d, s, q], r2.at[d, s, q], right if d == 0 else left)

    for q in range(CUTS):
        for d in range(2):
            gather_copy(d, 0, q).start()
    later = []
    for d in range(1, nf):
        copy = remote(feat_ref, fb_ref.at[mine], s3.at[d - 1], r3.at[d - 1], fpeers[d - 1])
        copy.start()
        later.append(copy)

    def fold(v):
        begin(v + 1)
        for d in range(2):
            fetch(d, v).wait()
            acc[...] += jnp.dot(
                abuf[v % 2, d],
                all_ref[block_of(d, v), d * half:(d + 1) * half, :],
                preferred_element_type=F32,
            )

    acc[...] = all_ref[me].astype(F32)
    fold(0)

    def gather_step(s, carry):
        for q in range(CUTS):
            for d in range(2):
                gather_copy(d, s - 1, q).wait_recv()
                gather_copy(d, s, q).start()
        fold(s)
        return carry

    lax.fori_loop(1, n - 1, gather_step, 0)
    for q in range(CUTS):
        for d in range(2):
            gather_copy(d, n - 2, q).wait_recv()
    fold(n - 1)

    for t in range(rows // tile):
        part = slice(t * tile, (t + 1) * tile)
        scale = sc_ref[part, :]
        v = scale * acc[part, :]
        square = v * v
        th = jnp.tanh(GELU_C * (v + GELU_A * (square * v)))
        level = 0.5 * (1.0 + th)
        out_ref[part, :] = (v * level).astype(BF16)
        slope = level + 0.5 * v * (1.0 - th * th) * (GELU_C * (1.0 + 3.0 * GELU_A * square))
        gt[:, part] = (scale * (slope * cot_ref[part, :].astype(F32))).T.astype(BF16)

    strip = cols // CUTS

    def scatter_copy(src, d, s, q):
        return remote(src, land.at[d, s, q], s4.at[d, s, q], r4.at[d, s, q], right if d == 0 else left)

    def term(v, d):
        fetch(d, v).wait()
        return jnp.dot(gt[...], abuf[v % 2, d], preferred_element_type=F32)

    begin(n + 1)
    for d in range(2):
        value = term(n, d).astype(BF16)
        for q in range(CUTS):
            stage[d, q] = value[q * strip:(q + 1) * strip]
            scatter_copy(stage.at[d, q], d, 0, q).start()

    def scatter_step(s, carry):
        begin(n + s + 1)
        for d in range(2):
            tbuf[d] = term(n + s, d)
        for q in range(CUTS):
            for d in range(2):
                slot = land.at[d, s - 1, q]
                scatter_copy(slot, d, s - 1, q).wait_recv()
                slot[...] = (slot[...].astype(F32) + tbuf[d, q * strip:(q + 1) * strip, :]).astype(BF16)
                scatter_copy(slot, d, s, q).start()
        return carry

    lax.fori_loop(1, n - 1, scatter_step, 0)
    for d in range(2):
        tbuf[d] = term(2 * n - 1, d) + gt[:, d * half:(d + 1) * half].astype(F32)
    for q in range(CUTS):
        for d in range(2):
            slot = land.at[d, n - 2, q]
            scatter_copy(slot, d, n - 2, q).wait_recv()
            part = slice(d * half, (d + 1) * half)
            total = slot[...].astype(F32) + tbuf[d, q * strip:(q + 1) * strip, :]
            tbuf[d, q * strip:(q + 1) * strip, :] = total * sct_ref[0:1, part]
    for t in range(rows // tile):
        d, at = t * tile // half, t * tile % half
        total = tbuf[d, :, at:at + tile]
        hgt[:, t * tile:(t + 1) * tile] = total.astype(BF16)
        hg[t * tile:(t + 1) * tile, :] = total.T.astype(BF16)

    sent = []
    for d in (2, 3, 1):
        peer = fpeers[d - 1]
        src = hg.at[pl.ds(pl.multiple_of(peer[1] * quarter, quarter), quarter)]
        copy = remote(src, hg4.at[mf], s5.at[d - 1], r5.at[d - 1], peer)
        copy.start()
        sent.append(copy)
    hg4[mf] = hg[mine, :]
    for copy in later:
        copy.wait_recv()
    wgt = jnp.dot(hgt[...], fb_ref[...], preferred_element_type=F32)
    wbuf[...] = wgt.T.astype(BF16)
    piece = wsum.shape[0]

    def piece_of(b):
        return pl.ds(pl.multiple_of(b * piece, piece), piece)

    pieces = []
    for d in range(1, n):
        peer = bpeers[d - 1]
        copy = remote(wbuf.at[piece_of(peer[0])], wland.at[d - 1], s6.at[d - 1], r6.at[d - 1], peer)
        copy.start()
        pieces.append(copy)
    summed = wbuf[piece_of(me), :].astype(F32)
    for d in range(1, n):
        pieces[d - 1].wait_recv()
        summed = summed + wland[d - 1].astype(F32)
    wsum[...] = summed.astype(BF16)
    finals = []
    for d in range(1, n):
        copy = remote(wsum, wfin.at[piece_of(me)], s7.at[d - 1], r7.at[d - 1], bpeers[d - 1])
        copy.start()
        finals.append(copy)
    wfin[piece_of(me), :] = wsum[...]
    for copy in sent:
        copy.wait_recv()
    total = None
    for f in range(nf):
        part = lax.dot_general(
            hg4[f], w_ref[:, f * cols:(f + 1) * cols], (((1,), (1,)), ((), ())),
            preferred_element_type=F32,
        )
        total = part if total is None else total + part
    gf_ref[...] = total.astype(BF16)

    def drain(s, carry):
        for q in range(CUTS):
            for d in range(2):
                gather_copy(d, s, q).wait_send()
                scatter_copy(land.at[d, s, q], d, s, q).wait_send()
        return carry

    lax.fori_loop(0, n - 1, drain, 0)
    for copy in first + later + sent + pieces:
        copy.wait_send()
    for copy in finals:
        copy.wait_recv()
    for copy in finals:
        copy.wait_send()


def finish_kernel(factor, out_in, gf_in, w_in, out_ref, gf_ref, gw_ref):
    out_ref[...] = out_in[...]
    gf_ref[...] = gf_in[...]
    gw_ref[...] = w_in[...].astype(F32) * factor


def per_device(features, weight, tile_vals, pair_counts, slot_row, slot_col, cotangent):
    n = lax.axis_size("blk")
    nf = lax.axis_size("feat")
    tiles = tile_vals[0]
    slots, tile, _ = tiles.shape
    cap = slots // n
    rows, cols = cotangent.shape
    quarter, width = features.shape
    tiles_row = rows // tile
    half = rows // 2
    dma = pltpu.SemaphoreType.DMA
    shape = jax.ShapeDtypeStruct

    dense, sc, sct = pl.pallas_call(
        functools.partial(dense_kernel, n, cap, tiles_row),
        grid_spec=pltpu.PrefetchScalarGridSpec(
            num_scalar_prefetch=3,
            grid=(n,),
            in_specs=[pl.BlockSpec((cap, tile, tile), lambda i, *_: (i, 0, 0))],
            out_specs=[
                pl.BlockSpec((1, 2, rows, half), lambda i, *_: (i, 0, 0, 0)),
                pl.BlockSpec((rows, tile), lambda i, *_: (0, 0)),
                pl.BlockSpec((8, rows), lambda i, *_: (0, 0)),
            ],
            scratch_shapes=[pltpu.VMEM((tiles_row, tile, tile), F32)],
        ),
        out_shape=[shape((n, 2, rows, half), BF16), shape((rows, tile), F32), shape((8, rows), F32)],
        compiler_params=pltpu.CompilerParams(
            dimension_semantics=("arbitrary",), vmem_limit_bytes=LIMIT
        ),
        name="dense",
    )(pair_counts, slot_row, slot_col, tiles)

    ring = dma((2, n - 1, CUTS))
    peers, others = dma((nf - 1,)), dma((n - 1,))
    vmem = pltpu.VMEM
    output, grad_features, summed = pl.pallas_call(
        functools.partial(layer_kernel, n, nf, tile),
        out_shape=[shape((rows, cols), BF16), shape((quarter, width), BF16), shape((width, cols), BF16)],
        in_specs=[VMEM] * 5 + [pl.BlockSpec(memory_space=pl.ANY)],
        out_specs=[VMEM] * 3,
        scratch_shapes=[
            vmem((n, rows, cols), BF16),
            vmem((rows, width), BF16),
            vmem((nf - 1, quarter, cols), BF16),
            vmem((2, 2, rows, half), BF16),
            vmem((rows, cols), F32),
            vmem((cols, rows), BF16),
            vmem((2, CUTS, cols // CUTS, half), BF16),
            vmem((2, cols, half), F32),
            vmem((2, n - 1, CUTS, cols // CUTS, half), BF16),
            vmem((cols, rows), BF16),
            vmem((rows, cols), BF16),
            vmem((nf, quarter, cols), BF16),
            vmem((width, cols), BF16),
            vmem((n - 1, width // n, cols), BF16),
            vmem((width // n, cols), BF16),
            dma((2, 2)),
            peers, peers, ring, ring, peers, peers, ring, ring, peers, peers,
            others, others, others, others,
        ],
        compiler_params=pltpu.CompilerParams(
            collective_id=0, has_side_effects=True, vmem_limit_bytes=LIMIT
        ),
        name="layer",
    )(features, weight, sc, sct, cotangent, dense)

    return tuple(
        pl.pallas_call(
            functools.partial(finish_kernel, (rows * n) ** (-0.5)),
            out_shape=[shape((rows, cols), BF16), shape((quarter, width), BF16), shape((width, cols), F32)],
            in_specs=[VMEM] * 3,
            out_specs=[VMEM] * 3,
            name="finish",
        )(output, grad_features, summed)
    )


def solution(mesh):
    in_specs = (
        P(("blk", "feat"), None),
        P(),
        P("blk", None, None, None),
        P("blk", None),
        P("blk", None),
        P("blk", None),
        P("blk", "feat"),
    )
    out_specs = (P("blk", "feat"), P(("blk", "feat"), None), P(None, "feat"))
    return jax.shard_map(
        per_device, mesh=mesh, in_specs=in_specs, out_specs=out_specs, check_vma=False
    )
```

```python
import functools

import jax
import jax.numpy as jnp
from jax import lax
from jax.experimental import pallas as pl
from jax.experimental.pallas import tpu as pltpu
from jax.sharding import PartitionSpec as P

MESH = pl.DeviceIdType.MESH
VMEM = pl.BlockSpec(memory_space=pltpu.VMEM)
F32, BF16 = jnp.float32, jnp.bfloat16
LIMIT = 56 * 1024 * 1024
CUTS = 4
GELU_C = 0.7978845608028654
GELU_A = 0.044715


def ring_of(n):
    me = lax.axis_index("blk")
    half = n // 2
    pos = jnp.where(me % 2 == 0, me // 2, n - 1 - me // 2)

    def blk_of(p):
        p = (p + 2 * n) % n
        return jnp.where(p < half, 2 * p, 2 * (n - 1 - p) + 1)

    return me, pos, blk_of


def greet(peers):
    barrier = pltpu.get_barrier_semaphore()
    for peer in peers:
        pl.semaphore_signal(barrier, inc=1, device_id=peer, device_id_type=MESH)
    pl.semaphore_wait(barrier, len(peers))


def remote(src, dst, send, recv, peer):
    return pltpu.make_async_remote_copy(
        src_ref=src, dst_ref=dst, send_sem=send, recv_sem=recv, device_id=peer, device_id_type=MESH
    )


def dense_kernel(n, cap, tiles_row, cnt_ref, row_ref, col_ref, tiles_ref, dense_ref, sc_ref, sct_ref, acc):
    c = pl.program_id(0)
    tile = tiles_ref.shape[1]
    across = tiles_row // 2

    @pl.when(c == 0)
    def _():
        acc[...] = jnp.zeros_like(acc)

    dense_ref[...] = jnp.zeros_like(dense_ref)
    count = cnt_ref[0, c]
    for k in range(cap):

        @pl.when(k < count)
        def _():
            row, col = row_ref[0, c * cap + k], col_ref[0, c * cap + k]
            value = tiles_ref[k]
            acc[row] += value.astype(F32)
            rows_at = pl.ds(pl.multiple_of(row * tile, tile), tile)
            cols_at = pl.ds(pl.multiple_of(col % across * tile, tile), tile)
            dense_ref[0, col // across, rows_at, cols_at] += value

    @pl.when(c == n - 1)
    def _():
        for t in range(tiles_row):
            degree = 1.0 + jnp.sum(acc[t], axis=1, keepdims=True)
            wide = jnp.broadcast_to(lax.rsqrt(degree), acc.shape[1:])
            sc_ref[t * tile:(t + 1) * tile, :] = wide
            sct_ref[:, t * tile:(t + 1) * tile] = wide.T[0:8]


def layer_kernel(
    n, nf, tile, feat_ref, w_ref, sc_ref, sct_ref, cot_ref, dense_ref, out_ref, gf_ref, wfin,
    all_ref, fb_ref, buf, abuf, acc, gt, stage, tbuf, land, hgt, hg, hg4, wbuf, wland, wsum,
    asem, s1, r1, s2, r2, s3, r3, s4, r4, s5, r5, s6, r6, s7, r7,
):
    me, pos, blk_of = ring_of(n)
    mf = lax.axis_index("feat")
    quarter = feat_ref.shape[0]
    rows, cols = all_ref.shape[1:]
    half = rows // 2
    right, left = (blk_of(pos + 1), mf), (blk_of(pos - 1), mf)
    fpeers = [(me, (mf + d) % nf) for d in range(1, nf)]
    bpeers = [((me + d) % n, mf) for d in range(1, n)]
    greet(fpeers + bpeers)

    def block_of(d, u):
        return blk_of(pos - u) if d == 0 else blk_of(pos + u)

    def fetch(d, v):
        u = jnp.where(v < n, v, v - n + 1)
        slot = v % 2
        return pltpu.make_async_copy(dense_ref.at[block_of(d, u), d], abuf.at[slot, d], asem.at[slot, d])

    def begin(v):
        for d in range(2):
            fetch(d, v).start()

    begin(0)
    mine = pl.ds(pl.multiple_of(mf * quarter, quarter), quarter)
    scale = sc_ref[mine, :]

    def rows_for(f):
        w = w_ref[:, pl.ds(pl.multiple_of(f * cols, cols), cols)]
        h = jnp.dot(feat_ref[...], w, preferred_element_type=F32)
        return (scale * h).astype(BF16)

    first = []
    for d in (2, 3, 1):
        peer = fpeers[d - 1]
        buf[d - 1] = rows_for(peer[1])
        copy = remote(buf.at[d - 1], all_ref.at[me, mine], s1.at[d - 1], r1.at[d - 1], peer)
        copy.start()
        first.append(copy)
    all_ref[me, mine, :] = rows_for(mf)
    fb_ref[mine, :] = feat_ref[...]
    chunk = half // CUTS

    def gather_copy(d, s, q):
        part = all_ref.at[block_of(d, s), pl.ds(d * half + q * chunk, chunk)]
        return remote(part, part, s2.at[d, s, q], r2.at[d, s, q], right if d == 0 else left)

    def start_quarter(f):
        for j in range(quarter // chunk):
            place = f * (quarter // chunk) + j
            d, q = place // CUTS, place % CUTS
            part = all_ref.at[me, pl.ds(pl.multiple_of(place * chunk, chunk), chunk)]
            remote(part, part, s2.at[d, 0, q], r2.at[d, 0, q], (blk_of(pos + 1 - 2 * d), mf)).start()

    start_quarter(mf)
    for copy, d in zip(first, (2, 3, 1)):
        copy.wait_recv()
        start_quarter((mf + nf - d) % nf)
    later = []
    for d in range(1, nf):
        copy = remote(feat_ref, fb_ref.at[mine], s3.at[d - 1], r3.at[d - 1], fpeers[d - 1])
        copy.start()
        later.append(copy)

    def fold(v):
        begin(v + 1)
        for d in range(2):
            fetch(d, v).wait()
            acc[...] += jnp.dot(
                abuf[v % 2, d],
                all_ref[block_of(d, v), d * half:(d + 1) * half, :],
                preferred_element_type=F32,
            )

    acc[...] = all_ref[me].astype(F32)
    fold(0)

    def gather_step(s, carry):
        for q in range(CUTS):
            for d in range(2):
                gather_copy(d, s - 1, q).wait_recv()
                gather_copy(d, s, q).start()
        fold(s)
        return carry

    lax.fori_loop(1, n - 1, gather_step, 0)
    for q in range(CUTS):
        for d in range(2):
            gather_copy(d, n - 2, q).wait_recv()
    fold(n - 1)

    for t in range(rows // tile):
        part = slice(t * tile, (t + 1) * tile)
        scale = sc_ref[part, :]
        v = scale * acc[part, :]
        square = v * v
        th = jnp.tanh(GELU_C * (v + GELU_A * (square * v)))
        level = 0.5 * (1.0 + th)
        out_ref[part, :] = (v * level).astype(BF16)
        slope = level + 0.5 * v * (1.0 - th * th) * (GELU_C * (1.0 + 3.0 * GELU_A * square))
        gt[:, part] = (scale * (slope * cot_ref[part, :].astype(F32))).T.astype(BF16)

    strip = cols // CUTS

    def scatter_copy(src, d, s, q):
        return remote(src, land.at[d, s, q], s4.at[d, s, q], r4.at[d, s, q], right if d == 0 else left)

    def term(v, d):
        fetch(d, v).wait()
        return jnp.dot(gt[...], abuf[v % 2, d], preferred_element_type=F32)

    begin(n + 1)
    for d in range(2):
        value = term(n, d).astype(BF16)
        for q in range(CUTS):
            stage[d, q] = value[q * strip:(q + 1) * strip]
            scatter_copy(stage.at[d, q], d, 0, q).start()

    def scatter_step(s, carry):
        begin(n + s + 1)
        for d in range(2):
            tbuf[d] = term(n + s, d)
        for q in range(CUTS):
            for d in range(2):
                slot = land.at[d, s - 1, q]
                scatter_copy(slot, d, s - 1, q).wait_recv()
                slot[...] = (slot[...].astype(F32) + tbuf[d, q * strip:(q + 1) * strip, :]).astype(BF16)
                scatter_copy(slot, d, s, q).start()
        return carry

    lax.fori_loop(1, n - 1, scatter_step, 0)
    for d in range(2):
        tbuf[d] = term(2 * n - 1, d) + gt[:, d * half:(d + 1) * half].astype(F32)
    for q in range(CUTS):
        for d in range(2):
            slot = land.at[d, n - 2, q]
            scatter_copy(slot, d, n - 2, q).wait_recv()
            part = slice(d * half, (d + 1) * half)
            total = slot[...].astype(F32) + tbuf[d, q * strip:(q + 1) * strip, :]
            tbuf[d, q * strip:(q + 1) * strip, :] = total * sct_ref[0:1, part]
    for t in range(rows // tile):
        d, at = t * tile // half, t * tile % half
        total = tbuf[d, :, at:at + tile]
        hgt[:, t * tile:(t + 1) * tile] = total.astype(BF16)
        hg[t * tile:(t + 1) * tile, :] = total.T.astype(BF16)

    sent = []
    for d in (2, 3, 1):
        peer = fpeers[d - 1]
        src = hg.at[pl.ds(pl.multiple_of(peer[1] * quarter, quarter), quarter)]
        copy = remote(src, hg4.at[mf], s5.at[d - 1], r5.at[d - 1], peer)
        copy.start()
        sent.append(copy)
    hg4[mf] = hg[mine, :]
    for copy in later:
        copy.wait_recv()
    wgt = jnp.dot(hgt[...], fb_ref[...], preferred_element_type=F32)
    wbuf[...] = wgt.T.astype(BF16)
    piece = wsum.shape[0]

    def piece_of(b):
        return pl.ds(pl.multiple_of(b * piece, piece), piece)

    pieces = []
    for d in range(1, n):
        peer = bpeers[d - 1]
        copy = remote(wbuf.at[piece_of(peer[0])], wland.at[d - 1], s6.at[d - 1], r6.at[d - 1], peer)
        copy.start()
        pieces.append(copy)
    summed = wbuf[piece_of(me), :].astype(F32)
    for d in range(1, n):
        pieces[d - 1].wait_recv()
        summed = summed + wland[d - 1].astype(F32)
    wsum[...] = summed.astype(BF16)
    finals = []
    for d in range(1, n):
        copy = remote(wsum, wfin.at[piece_of(me)], s7.at[d - 1], r7.at[d - 1], bpeers[d - 1])
        copy.start()
        finals.append(copy)
    wfin[piece_of(me), :] = wsum[...]
    for copy in sent:
        copy.wait_recv()
    total = None
    for f in range(nf):
        part = lax.dot_general(
            hg4[f], w_ref[:, f * cols:(f + 1) * cols], (((1,), (1,)), ((), ())),
            preferred_element_type=F32,
        )
        total = part if total is None else total + part
    gf_ref[...] = total.astype(BF16)

    def drain(s, carry):
        for q in range(CUTS):
            for d in range(2):
                gather_copy(d, s, q).wait_send()
                scatter_copy(land.at[d, s, q], d, s, q).wait_send()
        return carry

    lax.fori_loop(0, n - 1, drain, 0)
    for copy in first + later + sent + pieces:
        copy.wait_send()
    for copy in finals:
        copy.wait_recv()
    for copy in finals:
        copy.wait_send()


def finish_kernel(factor, out_in, gf_in, w_in, out_ref, gf_ref, gw_ref):
    out_ref[...] = out_in[...]
    gf_ref[...] = gf_in[...]
    gw_ref[...] = w_in[...].astype(F32) * factor


def per_device(features, weight, tile_vals, pair_counts, slot_row, slot_col, cotangent):
    n = lax.axis_size("blk")
    nf = lax.axis_size("feat")
    tiles = tile_vals[0]
    slots, tile, _ = tiles.shape
    cap = slots // n
    rows, cols = cotangent.shape
    quarter, width = features.shape
    tiles_row = rows // tile
    half = rows // 2
    dma = pltpu.SemaphoreType.DMA
    shape = jax.ShapeDtypeStruct

    dense, sc, sct = pl.pallas_call(
        functools.partial(dense_kernel, n, cap, tiles_row),
        grid_spec=pltpu.PrefetchScalarGridSpec(
            num_scalar_prefetch=3,
            grid=(n,),
            in_specs=[pl.BlockSpec((cap, tile, tile), lambda i, *_: (i, 0, 0))],
            out_specs=[
                pl.BlockSpec((1, 2, rows, half), lambda i, *_: (i, 0, 0, 0)),
                pl.BlockSpec((rows, tile), lambda i, *_: (0, 0)),
                pl.BlockSpec((8, rows), lambda i, *_: (0, 0)),
            ],
            scratch_shapes=[pltpu.VMEM((tiles_row, tile, tile), F32)],
        ),
        out_shape=[shape((n, 2, rows, half), BF16), shape((rows, tile), F32), shape((8, rows), F32)],
        compiler_params=pltpu.CompilerParams(
            dimension_semantics=("arbitrary",), vmem_limit_bytes=LIMIT
        ),
        name="dense",
    )(pair_counts, slot_row, slot_col, tiles)

    ring = dma((2, n - 1, CUTS))
    peers, others = dma((nf - 1,)), dma((n - 1,))
    vmem = pltpu.VMEM
    output, grad_features, summed = pl.pallas_call(
        functools.partial(layer_kernel, n, nf, tile),
        out_shape=[shape((rows, cols), BF16), shape((quarter, width), BF16), shape((width, cols), BF16)],
        in_specs=[VMEM] * 5 + [pl.BlockSpec(memory_space=pl.ANY)],
        out_specs=[VMEM] * 3,
        scratch_shapes=[
            vmem((n, rows, cols), BF16),
            vmem((rows, width), BF16),
            vmem((nf - 1, quarter, cols), BF16),
            vmem((2, 2, rows, half), BF16),
            vmem((rows, cols), F32),
            vmem((cols, rows), BF16),
            vmem((2, CUTS, cols // CUTS, half), BF16),
            vmem((2, cols, half), F32),
            vmem((2, n - 1, CUTS, cols // CUTS, half), BF16),
            vmem((cols, rows), BF16),
            vmem((rows, cols), BF16),
            vmem((nf, quarter, cols), BF16),
            vmem((width, cols), BF16),
            vmem((n - 1, width // n, cols), BF16),
            vmem((width // n, cols), BF16),
            dma((2, 2)),
            peers, peers, ring, ring, peers, peers, ring, ring, peers, peers,
            others, others, others, others,
        ],
        compiler_params=pltpu.CompilerParams(
            collective_id=0, has_side_effects=True, vmem_limit_bytes=LIMIT
        ),
        name="layer",
    )(features, weight, sc, sct, cotangent, dense)

    return tuple(
        pl.pallas_call(
            functools.partial(finish_kernel, (rows * n) ** (-0.5)),
            out_shape=[shape((rows, cols), BF16), shape((quarter, width), BF16), shape((width, cols), F32)],
            in_specs=[VMEM] * 3,
            out_specs=[VMEM] * 3,
            name="finish",
        )(output, grad_features, summed)
    )


def solution(mesh):
    in_specs = (
        P(("blk", "feat"), None),
        P(),
        P("blk", None, None, None),
        P("blk", None),
        P("blk", None),
        P("blk", None),
        P("blk", "feat"),
    )
    out_specs = (P("blk", "feat"), P(("blk", "feat"), None), P(None, "feat"))
    return jax.shard_map(
        per_device, mesh=mesh, in_specs=in_specs, out_specs=out_specs, check_vma=False
    )
```

```python
import functools

import jax
import jax.numpy as jnp
from jax import lax
from jax.experimental import pallas as pl
from jax.experimental.pallas import tpu as pltpu
from jax.sharding import PartitionSpec as P

MESH = pl.DeviceIdType.MESH
VMEM = pl.BlockSpec(memory_space=pltpu.VMEM)
F32, BF16 = jnp.float32, jnp.bfloat16
LIMIT = 56 * 1024 * 1024
CUTS = 4
GELU_C = 0.7978845608028654
GELU_A = 0.044715


def ring_of(n):
    me = lax.axis_index("blk")
    half = n // 2
    pos = jnp.where(me % 2 == 0, me // 2, n - 1 - me // 2)

    def blk_of(p):
        p = (p + 2 * n) % n
        return jnp.where(p < half, 2 * p, 2 * (n - 1 - p) + 1)

    return me, pos, blk_of


def greet(peers):
    barrier = pltpu.get_barrier_semaphore()
    for peer in peers:
        pl.semaphore_signal(barrier, inc=1, device_id=peer, device_id_type=MESH)
    return lambda: pl.semaphore_wait(barrier, len(peers))


def remote(src, dst, send, recv, peer):
    return pltpu.make_async_remote_copy(
        src_ref=src, dst_ref=dst, send_sem=send, recv_sem=recv, device_id=peer, device_id_type=MESH
    )


def dense_kernel(n, cap, tiles_row, cnt_ref, row_ref, col_ref, tiles_ref, dense_ref, sc_ref, sct_ref, acc):
    c = pl.program_id(0)
    tile = tiles_ref.shape[1]
    across = tiles_row // 2

    @pl.when(c == 0)
    def _():
        acc[...] = jnp.zeros_like(acc)

    dense_ref[...] = jnp.zeros_like(dense_ref)
    count = cnt_ref[0, c]
    for k in range(cap):

        @pl.when(k < count)
        def _():
            row, col = row_ref[0, c * cap + k], col_ref[0, c * cap + k]
            value = tiles_ref[k]
            acc[row] += value.astype(F32)
            rows_at = pl.ds(pl.multiple_of(row * tile, tile), tile)
            cols_at = pl.ds(pl.multiple_of(col % across * tile, tile), tile)
            dense_ref[0, col // across, rows_at, cols_at] += value

    @pl.when(c == n - 1)
    def _():
        for t in range(tiles_row):
            degree = 1.0 + jnp.sum(acc[t], axis=1, keepdims=True)
            wide = jnp.broadcast_to(lax.rsqrt(degree), acc.shape[1:])
            sc_ref[t * tile:(t + 1) * tile, :] = wide
            sct_ref[:, t * tile:(t + 1) * tile] = wide.T[0:8]


def layer_kernel(
    n, nf, tile, feat_ref, w_ref, sc_ref, sct_ref, cot_ref, dense_ref, out_ref, gf_ref, wfin,
    all_ref, fb_ref, buf, abuf, acc, gt, stage, tbuf, land, hgt, hg, hg4, wbuf, wland, wsum,
    asem, s1, r1, s2, r2, s3, r3, s4, r4, s5, r5, s6, r6, s7, r7,
):
    me, pos, blk_of = ring_of(n)
    mf = lax.axis_index("feat")
    quarter = feat_ref.shape[0]
    rows, cols = all_ref.shape[1:]
    half = rows // 2
    right, left = (blk_of(pos + 1), mf), (blk_of(pos - 1), mf)
    fpeers = [(me, (mf + d) % nf) for d in range(1, nf)]
    bpeers = [((me + d) % n, mf) for d in range(1, n)]
    all_here = greet(fpeers + bpeers)

    def block_of(d, u):
        return blk_of(pos - u) if d == 0 else blk_of(pos + u)

    def fetch(d, v):
        u = jnp.where(v < n, v, v - n + 1)
        slot = v % 2
        return pltpu.make_async_copy(dense_ref.at[block_of(d, u), d], abuf.at[slot, d], asem.at[slot, d])

    def begin(v):
        for d in range(2):
            fetch(d, v).start()

    begin(0)
    mine = pl.ds(pl.multiple_of(mf * quarter, quarter), quarter)
    scale = sc_ref[mine, :]

    def rows_for(f):
        w = w_ref[:, pl.ds(pl.multiple_of(f * cols, cols), cols)]
        h = jnp.dot(feat_ref[...], w, preferred_element_type=F32)
        return (scale * h).astype(BF16)

    for d in (2, 3, 1):
        buf[d - 1] = rows_for(fpeers[d - 1][1])
    all_ref[me, mine, :] = rows_for(mf)
    fb_ref[mine, :] = feat_ref[...]
    all_here()
    first = []
    for d in (2, 3, 1):
        peer = fpeers[d - 1]
        copy = remote(buf.at[d - 1], all_ref.at[me, mine], s1.at[d - 1], r1.at[d - 1], peer)
        copy.start()
        first.append(copy)
    for copy in first:
        copy.wait_recv()

    chunk = half // CUTS

    def gather_copy(d, s, q):
        part = all_ref.at[block_of(d, s), pl.ds(d * half + q * chunk, chunk)]
        return remote(part, part, s2.at[d, s, q], r2.at[d, s, q], right if d == 0 else left)

    for q in range(CUTS):
        for d in range(2):
            gather_copy(d, 0, q).start()
    later = []
    for d in range(1, nf):
        copy = remote(feat_ref, fb_ref.at[mine], s3.at[d - 1], r3.at[d - 1], fpeers[d - 1])
        copy.start()
        later.append(copy)

    def fold(v):
        begin(v + 1)
        for d in range(2):
            fetch(d, v).wait()
            acc[...] += jnp.dot(
                abuf[v % 2, d],
                all_ref[block_of(d, v), d * half:(d + 1) * half, :],
                preferred_element_type=F32,
            )

    acc[...] = all_ref[me].astype(F32)
    fold(0)

    def gather_step(s, carry):
        for q in range(CUTS):
            for d in range(2):
                gather_copy(d, s - 1, q).wait_recv()
                gather_copy(d, s, q).start()
        fold(s)
        return carry

    lax.fori_loop(1, n - 1, gather_step, 0)
    for q in range(CUTS):
        for d in range(2):
            gather_copy(d, n - 2, q).wait_recv()
    fold(n - 1)

    for t in range(rows // tile):
        part = slice(t * tile, (t + 1) * tile)
        scale = sc_ref[part, :]
        v = scale * acc[part, :]
        square = v * v
        th = jnp.tanh(GELU_C * (v + GELU_A * (square * v)))
        level = 0.5 * (1.0 + th)
        out_ref[part, :] = (v * level).astype(BF16)
        slope = level + 0.5 * v * (1.0 - th * th) * (GELU_C * (1.0 + 3.0 * GELU_A * square))
        gt[:, part] = (scale * (slope * cot_ref[part, :].astype(F32))).T.astype(BF16)

    strip = cols // CUTS

    def scatter_copy(src, d, s, q):
        return remote(src, land.at[d, s, q], s4.at[d, s, q], r4.at[d, s, q], right if d == 0 else left)

    def term(v, d):
        fetch(d, v).wait()
        return jnp.dot(gt[...], abuf[v % 2, d], preferred_element_type=F32)

    begin(n + 1)
    for d in range(2):
        value = term(n, d).astype(BF16)
        for q in range(CUTS):
            stage[d, q] = value[q * strip:(q + 1) * strip]
            scatter_copy(stage.at[d, q], d, 0, q).start()

    def scatter_step(s, carry):
        begin(n + s + 1)
        for d in range(2):
            tbuf[d] = term(n + s, d)
        for q in range(CUTS):
            for d in range(2):
                slot = land.at[d, s - 1, q]
                scatter_copy(slot, d, s - 1, q).wait_recv()
                slot[...] = (slot[...].astype(F32) + tbuf[d, q * strip:(q + 1) * strip, :]).astype(BF16)
                scatter_copy(slot, d, s, q).start()
        return carry

    lax.fori_loop(1, n - 1, scatter_step, 0)
    for d in range(2):
        tbuf[d] = term(2 * n - 1, d) + gt[:, d * half:(d + 1) * half].astype(F32)
    for q in range(CUTS):
        for d in range(2):
            slot = land.at[d, n - 2, q]
            scatter_copy(slot, d, n - 2, q).wait_recv()
            part = slice(d * half, (d + 1) * half)
            total = slot[...].astype(F32) + tbuf[d, q * strip:(q + 1) * strip, :]
            tbuf[d, q * strip:(q + 1) * strip, :] = total * sct_ref[0:1, part]
    for t in range(rows // tile):
        d, at = t * tile // half, t * tile % half
        total = tbuf[d, :, at:at + tile]
        hgt[:, t * tile:(t + 1) * tile] = total.astype(BF16)
        hg[t * tile:(t + 1) * tile, :] = total.T.astype(BF16)

    sent = []
    for d in (2, 3, 1):
        peer = fpeers[d - 1]
        src = hg.at[pl.ds(pl.multiple_of(peer[1] * quarter, quarter), quarter)]
        copy = remote(src, hg4.at[mf], s5.at[d - 1], r5.at[d - 1], peer)
        copy.start()
        sent.append(copy)
    hg4[mf] = hg[mine, :]
    for copy in later:
        copy.wait_recv()
    wgt = jnp.dot(hgt[...], fb_ref[...], preferred_element_type=F32)
    wbuf[...] = wgt.T.astype(BF16)
    piece = wsum.shape[0]

    def piece_of(b):
        return pl.ds(pl.multiple_of(b * piece, piece), piece)

    pieces = []
    for d in range(1, n):
        peer = bpeers[d - 1]
        copy = remote(wbuf.at[piece_of(peer[0])], wland.at[d - 1], s6.at[d - 1], r6.at[d - 1], peer)
        copy.start()
        pieces.append(copy)
    summed = wbuf[piece_of(me), :].astype(F32)
    for d in range(1, n):
        pieces[d - 1].wait_recv()
        summed = summed + wland[d - 1].astype(F32)
    wsum[...] = summed.astype(BF16)
    finals = []
    for d in range(1, n):
        copy = remote(wsum, wfin.at[piece_of(me)], s7.at[d - 1], r7.at[d - 1], bpeers[d - 1])
        copy.start()
        finals.append(copy)
    wfin[piece_of(me), :] = wsum[...]
    for copy in sent:
        copy.wait_recv()
    total = None
    for f in range(nf):
        part = lax.dot_general(
            hg4[f], w_ref[:, f * cols:(f + 1) * cols], (((1,), (1,)), ((), ())),
            preferred_element_type=F32,
        )
        total = part if total is None else total + part
    gf_ref[...] = total.astype(BF16)

    def drain(s, carry):
        for q in range(CUTS):
            for d in range(2):
                gather_copy(d, s, q).wait_send()
                scatter_copy(land.at[d, s, q], d, s, q).wait_send()
        return carry

    lax.fori_loop(0, n - 1, drain, 0)
    for copy in first + later + sent + pieces:
        copy.wait_send()
    for copy in finals:
        copy.wait_recv()
    for copy in finals:
        copy.wait_send()


def finish_kernel(factor, out_in, gf_in, w_in, out_ref, gf_ref, gw_ref):
    out_ref[...] = out_in[...]
    gf_ref[...] = gf_in[...]
    gw_ref[...] = w_in[...].astype(F32) * factor


def per_device(features, weight, tile_vals, pair_counts, slot_row, slot_col, cotangent):
    n = lax.axis_size("blk")
    nf = lax.axis_size("feat")
    tiles = tile_vals[0]
    slots, tile, _ = tiles.shape
    cap = slots // n
    rows, cols = cotangent.shape
    quarter, width = features.shape
    tiles_row = rows // tile
    half = rows // 2
    dma = pltpu.SemaphoreType.DMA
    shape = jax.ShapeDtypeStruct

    dense, sc, sct = pl.pallas_call(
        functools.partial(dense_kernel, n, cap, tiles_row),
        grid_spec=pltpu.PrefetchScalarGridSpec(
            num_scalar_prefetch=3,
            grid=(n,),
            in_specs=[pl.BlockSpec((cap, tile, tile), lambda i, *_: (i, 0, 0))],
            out_specs=[
                pl.BlockSpec((1, 2, rows, half), lambda i, *_: (i, 0, 0, 0)),
                pl.BlockSpec((rows, tile), lambda i, *_: (0, 0)),
                pl.BlockSpec((8, rows), lambda i, *_: (0, 0)),
            ],
            scratch_shapes=[pltpu.VMEM((tiles_row, tile, tile), F32)],
        ),
        out_shape=[shape((n, 2, rows, half), BF16), shape((rows, tile), F32), shape((8, rows), F32)],
        compiler_params=pltpu.CompilerParams(
            dimension_semantics=("arbitrary",), vmem_limit_bytes=LIMIT
        ),
        name="dense",
    )(pair_counts, slot_row, slot_col, tiles)

    ring = dma((2, n - 1, CUTS))
    peers, others = dma((nf - 1,)), dma((n - 1,))
    vmem = pltpu.VMEM
    output, grad_features, summed = pl.pallas_call(
        functools.partial(layer_kernel, n, nf, tile),
        out_shape=[shape((rows, cols), BF16), shape((quarter, width), BF16), shape((width, cols), BF16)],
        in_specs=[VMEM] * 5 + [pl.BlockSpec(memory_space=pl.ANY)],
        out_specs=[VMEM] * 3,
        scratch_shapes=[
            vmem((n, rows, cols), BF16),
            vmem((rows, width), BF16),
            vmem((nf - 1, quarter, cols), BF16),
            vmem((2, 2, rows, half), BF16),
            vmem((rows, cols), F32),
            vmem((cols, rows), BF16),
            vmem((2, CUTS, cols // CUTS, half), BF16),
            vmem((2, cols, half), F32),
            vmem((2, n - 1, CUTS, cols // CUTS, half), BF16),
            vmem((cols, rows), BF16),
            vmem((rows, cols), BF16),
            vmem((nf, quarter, cols), BF16),
            vmem((width, cols), BF16),
            vmem((n - 1, width // n, cols), BF16),
            vmem((width // n, cols), BF16),
            dma((2, 2)),
            peers, peers, ring, ring, peers, peers, ring, ring, peers, peers,
            others, others, others, others,
        ],
        compiler_params=pltpu.CompilerParams(
            collective_id=0, has_side_effects=True, vmem_limit_bytes=LIMIT
        ),
        name="layer",
    )(features, weight, sc, sct, cotangent, dense)

    return tuple(
        pl.pallas_call(
            functools.partial(finish_kernel, (rows * n) ** (-0.5)),
            out_shape=[shape((rows, cols), BF16), shape((quarter, width), BF16), shape((width, cols), F32)],
            in_specs=[VMEM] * 3,
            out_specs=[VMEM] * 3,
            name="finish",
        )(output, grad_features, summed)
    )


def solution(mesh):
    in_specs = (
        P(("blk", "feat"), None),
        P(),
        P("blk", None, None, None),
        P("blk", None),
        P("blk", None),
        P("blk", None),
        P("blk", "feat"),
    )
    out_specs = (P("blk", "feat"), P(("blk", "feat"), None), P(None, "feat"))
    return jax.shard_map(
        per_device, mesh=mesh, in_specs=in_specs, out_specs=out_specs, check_vma=False
    )
```
